128 devices in a mesh: leaf: 128 (over y, x, z, core).
Axes of the slice: x: 4, y: 4, z: 4, core: 2. Of those that a mesh axis runs over, the one named last changes fastest.
Arguments:
- points: float32 [3, 524288], P(None, 'leaf'), may hold values from 0 to 1
- rhs: float32 [16, 524288], P(None, 'leaf'), may hold values from -6 to 6
- leaf_basis: float32 [32, 524288], P(None, 'leaf'), may hold values from -0.75 to 0.75
- transfer: float32 [32, 32, 10752], P(None, None, 'leaf'), may hold values from -0.5 to 0.5
- proxies: float32 [3, 32, 10880], P(None, None, 'leaf'), may hold values from 0 to 1
- near_list: int32 [8192, 5], P('leaf'), may hold values from -1 to 8191, as said below
- couple_list: int32 [10752, 20], P('leaf'), may hold values from -1 to 8191, as said below
- root_list: int32 [128, 128], P('leaf'), may hold values from -1 to 127, as said below
Outputs:
- product: float32 [16, 524288], P(None, 'leaf')
The draws below stay inside these ranges and needn't reach their ends.
Inputs may be any that keep to these rules, and one draw needn't show every extreme that they name: `near_list`: entry [t, j] is the leaf t + j - 2 if the block of leaves t and t + j - 2 is near, else -1; every leaf is near itself. Nearness is defined level by level: at level 0 roots t and s are near when they differ by at most a per-root reach of 1 to 2 (the larger of the two); below, two clusters are near when their parents are near and they differ by at most the larger of their reaches. Near leaf blocks, with the coupled pairs of the other two lists, cover every pair of points exactly once. `couple_list`: the row of a cluster t of level l lists in slot j the cluster s = 4 * (t // 4 - 2) + j of level l if s exists, the parents of t and s are near and t and s are not near, else -1. `root_list`: entry [t, s] is s if roots t and s are not near, else -1.
All inputs are finite; a program needn't handle non-finite values.
Results may differ from the reference program's by a relative error of at most 0.0003.
Values sent between devices are 32-bit elements; how exact they have to be, the bound alone decides.
A program may use at most 128 MiB of HBM per device.

```python
import math
import jax
import jax.numpy as jnp
from jax import lax

RANK = 32
NVEC = 16
LEAF = 64
LEVELS = 3
REACH = 2
FAR_SLOTS = 20
LEAF_DEV = 64
TR_DEV = 84
PX_DEV = 85
ROOTS = 128
LEAVES = 8192
NPTS = 524288
N_LEAF = 128


def closeness(key):
    masks = []
    for level_no in range(LEVELS + 1):
        clusters = ROOTS * 4 ** level_no
        reaches = jax.random.randint(jax.random.fold_in(key, 11 + level_no), (clusters,), 1, REACH + 1)
        target = jnp.arange(clusters, dtype=jnp.int32)[:, None]
        offset = jnp.arange(-REACH, REACH + 1, dtype=jnp.int32)[None, :]
        source = target + offset
        inside = (source >= 0) & (source < clusters)
        clipped = jnp.clip(source, 0, clusters - 1)
        is_near = inside & (jnp.abs(offset) <= jnp.maximum(reaches[:, None], reaches[clipped]))
        if level_no > 0:
            parent_rows = masks[-1][target[:, 0] // 4]
            column = jnp.clip(source // 4 - target // 4 + REACH, 0, 2 * REACH)
            is_near = is_near & jnp.take_along_axis(parent_rows, column, axis=1)
        masks.append(is_near)
    return masks


def far_entries(masks, level_no):
    clusters = ROOTS * 4 ** level_no
    target = jnp.arange(clusters, dtype=jnp.int32)[:, None]
    slot = jnp.arange(FAR_SLOTS, dtype=jnp.int32)[None, :]
    parent = target // 4
    source = 4 * (parent - REACH) + slot
    inside = (source >= 0) & (source < clusters)
    parent_close = jnp.take_along_axis(masks[level_no - 1][parent[:, 0]], jnp.broadcast_to(slot // 4, (clusters, FAR_SLOTS)), axis=1)
    gap = source - target
    own_close = jnp.take_along_axis(masks[level_no], jnp.clip(gap + REACH, 0, 2 * REACH), axis=1)
    is_close = (jnp.abs(gap) <= REACH) & own_close
    is_far = inside & parent_close & jnp.logical_not(is_close)
    return jnp.where(is_far, source, -1).astype(jnp.int32)


def draw_near_list(key, part):
    masks = closeness(jax.random.fold_in(key, 5))
    target = jnp.arange(ROOTS * LEAF_DEV, dtype=jnp.int32)[:, None]
    offset = jnp.arange(-REACH, REACH + 1, dtype=jnp.int32)[None, :]
    return jnp.where(masks[LEVELS], target + offset, -1).astype(jnp.int32)


def draw_couple_list(key, part):
    masks = closeness(jax.random.fold_in(key, 5))
    blocks = []
    for level_no in range(1, LEVELS + 1):
        blocks.append(far_entries(masks, level_no).reshape(ROOTS, 4 ** level_no, FAR_SLOTS))
    return jnp.concatenate(blocks, axis=1).reshape(ROOTS * TR_DEV, FAR_SLOTS)


def draw_root_list(key, part):
    masks = closeness(jax.random.fold_in(key, 5))
    target = jnp.arange(ROOTS, dtype=jnp.int32)[:, None]
    source = jnp.arange(ROOTS, dtype=jnp.int32)[None, :]
    gap = source - target
    own_close = jnp.take_along_axis(masks[0], jnp.clip(gap + REACH, 0, 2 * REACH), axis=1)
    is_close = (jnp.abs(gap) <= REACH) & own_close
    return jnp.where(is_close, -1, jnp.broadcast_to(source, (ROOTS, ROOTS))).astype(jnp.int32)


def block_scale(rng, shape, shards, low, top_value):
    def one(position, blocks):
        draws = jax.random.uniform(jax.random.fold_in(jax.random.fold_in(rng, 6), position), (blocks,), jnp.float32, low / len(shards), top_value / len(shards))
        return jnp.repeat(jnp.exp(draws), shape[position] // blocks).reshape((-1,) + (1,) * (len(shape) - position - 1))

    factor_of = one(*shards[0])
    for cut in shards[1:]:
        factor_of = factor_of * one(*cut)
    return factor_of


def scatter_about(own_key, shape, width, bound, cuts=(), kind=jnp.bfloat16):
    values = width * jax.random.normal(own_key, shape, jnp.float32)
    if cuts:
        values = values * block_scale(own_key, shape, cuts, -0.22, 0.18)
    return jnp.clip(values, -bound, bound).astype(kind)


def setup_inputs(seed: int = 0) -> dict:
    streams_of = jax.random.split(jax.random.key(seed), 9)
    return {
        "points": jnp.clip(1.0 * jax.random.uniform(streams_of[0], (3, NPTS), jnp.float32) ** block_scale(streams_of[0], (3, NPTS), ((1, 128),), -0.2, 0.2), 0.0, 1.0),
        "rhs": scatter_about(streams_of[1], (NVEC, NPTS), 1.0, 6.0, ((1, 128),), jnp.float32),
        "leaf_basis": scatter_about(streams_of[2], (RANK, NPTS), LEAF ** -0.5, 0.75, ((1, 128),), jnp.float32),
        "transfer": scatter_about(streams_of[3], (RANK, RANK, TR_DEV * N_LEAF), (4 * RANK) ** -0.5, 0.5, ((2, 128),), jnp.float32),
        "proxies": jnp.clip(1.0 * jax.random.uniform(streams_of[4], (3, RANK, PX_DEV * N_LEAF), jnp.float32) ** block_scale(streams_of[4], (3, RANK, PX_DEV * N_LEAF), ((2, 128),), -0.2, 0.2), 0.0, 1.0),
        "near_list": draw_near_list(jax.random.fold_in(streams_of[8], 71), 0),
        "couple_list": draw_couple_list(jax.random.fold_in(streams_of[8], 71), 0),
        "root_list": draw_root_list(jax.random.fold_in(streams_of[8], 71), 0),
    }


kernel_band = 0.1
highest = lax.Precision.HIGHEST


def kernel_sq(left_pts, right_pts):
    length = (left_pts[0] - right_pts[0]) ** 2 + (left_pts[1] - right_pts[1]) ** 2 + (left_pts[2] - right_pts[2]) ** 2
    return jnp.exp(-length / kernel_band)


def by_blocks(method, inputs, length, stride, out_shape):
    stride = math.gcd(length, stride)

    def advance(step_no, accumulated):
        begin_at = step_no * stride
        pieces = [lax.dynamic_slice_in_dim(operand, begin_at, stride, operand.ndim - 1) for operand in inputs]
        return lax.dynamic_update_slice_in_dim(accumulated, method(*pieces), begin_at, accumulated.ndim - 1)

    return lax.fori_loop(0, length // stride, advance, jnp.zeros(out_shape, jnp.float32))


def couple(target_prox, lookup, source_prox, listed):
    usable = listed.T >= 0
    clipped = jnp.where(usable, listed.T, 0)

    def one_block(target_blk, clipped_blk, usable_blk):
        coeff_blk = jnp.take(lookup, clipped_blk, axis=2)
        prox_blk = jnp.take(source_prox, clipped_blk, axis=2)
        kernel = kernel_sq(target_blk[:, :, None, None, :], prox_blk[:, None, :, :, :]) * usable_blk.astype(coeff_blk.dtype)
        return jnp.einsum('absn,bksn->akn', kernel, coeff_blk, precision=highest)

    extent = listed.shape[0]
    return by_blocks(one_block, [target_prox, clipped, usable], extent, 128, (lookup.shape[0], lookup.shape[1], extent))


def near_field(targets, lookup, listed, vectors):
    usable = listed.T >= 0
    clipped = jnp.where(usable, listed.T, 0)

    def one_block(target_blk, clipped_blk, usable_blk):
        source = jnp.take(lookup, clipped_blk, axis=2)
        kernel = kernel_sq(target_blk[:, :, None, None, :], source[vectors:, None, :, :, :]) * usable_blk.astype(source.dtype)
        return jnp.einsum('ijsn,kjsn->kin', kernel, source[:vectors], precision=highest)

    extent = listed.shape[0]
    return by_blocks(one_block, [targets, clipped, usable], extent, 128, (vectors, targets.shape[1], extent))


def reference(points, rhs, leaf_basis, transfer, proxies, near_list, couple_list, root_list):
    basis_grid = leaf_basis.reshape(RANK, LEAVES, LEAF)
    coeffs = [None] * (LEVELS + 1)
    coeffs[LEVELS] = jnp.einsum('rnp,knp->rkn', basis_grid, rhs.reshape(NVEC, LEAVES, LEAF), precision=highest)
    proxy_grid = proxies.reshape(3, RANK, ROOTS, PX_DEV)
    transfer_grid = transfer.reshape(RANK, RANK, ROOTS, TR_DEV)
    list_grid = couple_list.reshape(ROOTS, TR_DEV, FAR_SLOTS)
    level_prox = []
    mappings = [None]
    entries = [None]
    for level_no in range(LEVELS + 1):
        extent = 4 ** level_no
        begin_at = (extent - 1) // 3
        level_prox.append(proxy_grid[:, :, :, begin_at:begin_at + extent].reshape(3, RANK, ROOTS * extent))
        if level_no > 0:
            mappings.append(transfer_grid[:, :, :, begin_at - 1:begin_at - 1 + extent].reshape(RANK, RANK, ROOTS * extent))
            entries.append(list_grid[:, begin_at - 1:begin_at - 1 + extent].reshape(ROOTS * extent, FAR_SLOTS))
    for level_no in range(LEVELS, 0, -1):
        merged = jnp.einsum('abn,akn->bkn', mappings[level_no], coeffs[level_no], precision=highest)
        coeffs[level_no - 1] = merged.reshape(RANK, NVEC, -1, 4).sum(axis=3)
    coupled = []
    for level_no in range(LEVELS + 1):
        listed = root_list if level_no == 0 else entries[level_no]
        coupled.append(couple(level_prox[level_no], coeffs[level_no], level_prox[level_no], listed))
    downward = coupled[0]
    for level_no in range(1, LEVELS + 1):
        downward = coupled[level_no] + jnp.einsum('abn,bkn->akn', mappings[level_no], jnp.repeat(downward, 4, axis=2), precision=highest)
    lookup_pts = jnp.concatenate([rhs, points], axis=0).reshape(NVEC + 3, LEAVES, LEAF).transpose(0, 2, 1)
    targets = points.reshape(3, LEAVES, LEAF).transpose(0, 2, 1)
    near_part = near_field(targets, lookup_pts, near_list, NVEC)
    far_part = jnp.einsum('rnp,rkn->knp', basis_grid, downward, precision=highest)
    return (near_part.transpose(0, 2, 1) + far_part).reshape(NVEC, NPTS)
```

```python
import functools
import math

import jax
import jax.numpy as jnp
from jax import lax
from jax.experimental import pallas as pl
from jax.experimental.pallas import tpu as pltpu
from jax.sharding import PartitionSpec as P

F32, BF16 = jnp.float32, jnp.bfloat16
MESH = pl.DeviceIdType.MESH
BIG = 16384.0
SCALE = math.sqrt(10.0 * math.log2(math.e))
LANES = 128
KN = 64
KC = 80


def nt(a, b):
    return lax.dot_general(a, b, (((1,), (1,)), ((), ())), preferred_element_type=F32)


def nn(a, b):
    return lax.dot_general(a, b, (((1,), (0,)), ((), ())), preferred_element_type=F32)


def iota(shape, dim):
    return lax.broadcasted_iota(jnp.int32, shape, dim)


def halves(x):
    hi = x.astype(BF16)
    return hi, (x - hi.astype(F32)).astype(BF16)


def stacked(x):
    hi = x.astype(BF16).astype(F32)
    return jnp.concatenate([hi, x - hi], axis=0).astype(BF16)


def folded(x):
    n = x.shape[0] // 2
    return x[:n] + x[n:]


def thirds(x):
    h = x.astype(BF16).astype(F32)
    m = (x - h).astype(BF16).astype(F32)
    return h, m, x - h - m


def source_rows(x):
    r = iota(x.shape, 0)
    x = jnp.where(r < 3, x, 0.0)
    n2 = jnp.sum(x * x, axis=0, keepdims=True)
    return jnp.where(r < 3, x, jnp.where(r == 3, n2, jnp.where(r == 4, 1.0, 0.0)))


def target_rows(x):
    r = iota(x.shape, 0)
    x = jnp.where(r < 3, x, 0.0)
    n2 = jnp.sum(x * x, axis=0, keepdims=True)
    return jnp.where(r < 3, 2.0 * x, jnp.where(r == 3, -1.0, jnp.where(r == 4, -n2, 0.0)))


def source_stack(rows):
    h, m, l = thirds(rows)
    return [h, m, l, h, m, h]


def target_stack(rows):
    h, m, l = thirds(rows)
    return [h, h, h, m, m, l]


def gauss(e):
    g = jnp.exp2(e)
    return halves(g)


def kernel(
    n_dev,
    pts_ref, rhs_ref, basis_ref, tr_ref, px_ref, nl_ref, cl_ref, rl_ref,
    out_ref,
    p8, pa, tb, tbh, tbl, eye_ref, bmask,
    ytn, chn, xn, ytc, chc, xc, clb, nlb, rb,
    gc, fc,
    sn, rn, sl, rlr, s1, r1, sq, rq, rg,
    sem_s, sem_r, gs_sem, gr_sem,
):
    me = lax.axis_index("leaf")
    quads = n_dev // 4
    quad, seat = me // 4, me % 4
    left, right = (me + n_dev - 1) % n_dev, (me + 1) % n_dev
    left2, right2 = (me + n_dev - 2) % n_dev, (me + 2) % n_dev
    peers = [quad * 4 + (seat + o) % 4 for o in range(1, 4)]

    def dst(o):
        return ((quad + o) % quads) * 4 + seat

    barrier = pltpu.get_barrier_semaphore()
    for d in [left, right, left2, right2, *peers]:
        pl.semaphore_signal(barrier, inc=1, device_id=(d,), device_id_type=MESH)

    def greet(o, c):
        pl.semaphore_signal(barrier, inc=1, device_id=(dst(o),), device_id_type=MESH)
        return c

    lax.fori_loop(1, quads, greet, 0)

    p8[...] = jnp.zeros_like(p8)
    p8[0:3, :] = (pts_ref[...] - 0.5) * SCALE
    for i, u in ((0, 0), (1, 31)):
        sn[i, 0:16, :] = rhs_ref[:, u * LANES : (u + 1) * LANES]
        sn[i, 16:24, :] = source_rows(p8[:, u * LANES : (u + 1) * LANES])

    pl.semaphore_wait(barrier, 7 + quads - 1)

    def remote(src, dst_ref, i, d):
        return pltpu.make_async_remote_copy(
            src_ref=src, dst_ref=dst_ref, send_sem=sem_s.at[i], recv_sem=sem_r.at[i],
            device_id=(d,), device_id_type=MESH,
        )

    near_copies = [
        remote(sn.at[0], rn.at[1], 0, left),
        remote(sn.at[1], rn.at[0], 1, right),
    ]
    for c in near_copies:
        c.start()

    eye_ref[...] = jnp.where(iota((LANES, LANES), 0) == iota((LANES, LANES), 1), 1.0, 0.0).astype(BF16)
    bmask[...] = jnp.where(iota((LANES, 256), 0) // 32 == iota((LANES, 256), 1) // 64, 1.0, 0.0).astype(BF16)

    lane_n, row_n = iota((LANES, 84), 1), iota((LANES, 84), 0)
    tmask = (lane_n < 4) | (((lane_n >> 2) + 3) % 4 == (row_n >> 5))
    eye84 = jnp.where(iota((84, 84), 0) == iota((84, 84), 1), 1.0, 0.0).astype(BF16)

    def turn(a, c):
        w = tr_ref[a]
        w = jnp.where(tmask, jnp.concatenate([w, w, w, w], axis=0), 0.0)
        hi, lo = halves(w)
        tb[pl.ds(a, 84, stride=32), :] = nt(eye84, hi) + nt(eye84, lo)
        return c

    lax.fori_loop(0, 32, turn, 0)

    def part(i, c):
        hi, lo = halves(tb[pl.ds(i * LANES, LANES), :])
        tbh[i] = hi
        tbl[i] = lo
        return c

    lax.fori_loop(0, 21, part, 0)

    pick = jnp.where(
        ((iota((24, 85), 1) >= 1) & ((iota((24, 85), 1) - 1) >> 2 == iota((24, 85), 0)))
        | ((iota((24, 85), 1) == 0) & (iota((24, 85), 0) == 21)), 1.0, 0.0).astype(BF16)
    lane_p, row_p = iota((LANES, 85), 1), iota((LANES, 85), 0)
    pmask = (lane_p == 0) | ((lane_p + 3) % 4 == (row_p >> 5))
    pa[...] = jnp.zeros_like(pa)
    for ax in range(3):
        w = (px_ref[ax] - 0.5) * SCALE
        w = jnp.where(pmask, jnp.concatenate([w, w, w, w], axis=0), 0.0)
        h, m, l = thirds(w)
        pa[pl.ds(ax, 24, stride=8), :] = (
            nt(pick, h.astype(BF16)) + nt(pick, m.astype(BF16)) + nt(pick, l.astype(BF16))
        )

    def basis_parts(q):
        hi, lo = halves(basis_ref[:, pl.ds(q * 256, 256)])
        mask = bmask[...]
        return (
            jnp.concatenate([hi, hi, hi, hi], axis=0) * mask,
            jnp.concatenate([lo, lo, lo, lo], axis=0) * mask,
        )

    def place(level, q):
        return {1: 28, 2: 20, 3: 0}[level] + 2 + q, {1: 0, 2: 1, 3: 5}[level] + q

    coef3 = gc

    def leaf_coef(q, c):
        bh, bl = basis_parts(q)
        v = stacked(rhs_ref[:, pl.ds(q * 256, 256)])
        coef3[5 + q] = folded(nt(v, bh) + nt(v, bl))
        return c

    lax.fori_loop(0, 16, leaf_coef, 0)

    for r in range(4):
        acc = jnp.zeros((32, LANES), F32)
        for i in range(4):
            b = stacked(coef3[5 + 4 * r + i])
            acc += nn(b, tbh[5 + 4 * r + i]) + nn(b, tbl[5 + 4 * r + i])
        coef3[1 + r] = folded(acc)
    acc = jnp.zeros((32, LANES), F32)
    for i in range(4):
        b = stacked(coef3[1 + i])
        acc += nn(b, tbh[1 + i]) + nn(b, tbl[1 + i])
    coef3[0] = folded(acc)
    b = stacked(coef3[0])
    coef0 = folded(nn(b, tbh[0]) + nn(b, tbl[0]))

    sq[0:16, :] = coef0
    sq[16:24, :] = source_rows(pa[21 * 8 : 22 * 8, :])
    for i, (to_left, to_right) in enumerate(((5, 19), (6, 20), (1, 3), (2, 4), (0, 0))):
        for side, u in ((0, to_left), (1, to_right)):
            sl[side, i, 0:16, :] = coef3[u]
            sl[side, i, 16:24, :] = source_rows(pa[u * 8 : u * 8 + 8, :])
    s1[0:16, :] = coef3[0]
    s1[16:24, :] = source_rows(pa[0:8, :])
    rq[seat] = sq[...]
    quad_copies = [
        pltpu.make_async_remote_copy(
            src_ref=sq, dst_ref=rq.at[seat], send_sem=sem_s.at[6 + o], recv_sem=sem_r.at[6 + seat],
            device_id=(peers[o],), device_id_type=MESH,
        )
        for o in range(3)
    ]
    for c in quad_copies:
        c.start()
    level_copies = [
        remote(sl.at[0], rlr.at[1], 2, left),
        remote(sl.at[1], rlr.at[0], 3, right),
        remote(s1, r1.at[1], 4, left2),
        remote(s1, r1.at[0], 5, right2),
    ]
    for c in level_copies:
        c.start()

    clb[...] = jnp.full_like(clb, -BIG)
    clb[0:20, 0:84] = jnp.where(cl_ref[...] >= 0, 0.0, -BIG)
    nlb[...] = jnp.full_like(nlb, -BIG)
    nlb[0:5, 0:64] = jnp.where(nl_ref[...] >= 0, 0.0, -BIG)
    nb = nlb[...]
    nlb[...] = jnp.where(iota((8, LANES), 1) % 2 == 1, pltpu.roll(nb, 1, axis=0), nb)
    sel4 = jnp.where(iota((LANES, LANES), 0) == iota((LANES, LANES), 1) >> 5, 1.0, 0.0).astype(BF16)
    sel2 = jnp.where(iota((LANES, LANES), 0) == iota((LANES, LANES), 1) >> 6, 1.0, 0.0).astype(BF16)
    selm = jnp.where(iota((LANES, LANES), 0) % 4 == iota((LANES, LANES), 1) >> 5, 1.0, 0.0).astype(BF16)
    rlist = jnp.where(rl_ref[...] >= 0, 0.0, -BIG) + jnp.zeros((32, LANES), F32)
    rlist = jnp.where(iota((32, LANES), 1) >> 2 == iota((32, LANES), 0), rlist, 0.0)
    rb[...] = nn(rlist.astype(BF16), selm)

    def near_source(slab, values, rows):
        cls = (2 * slab + (iota((8, LANES), 1) >> 6)) % 8
        hot = jnp.where(iota((8, LANES), 0) == cls, 1.0, 0.0)
        f = jnp.concatenate([*source_stack(rows), hot, jnp.zeros((8, LANES), F32)], axis=0)
        ytn[pl.ds(pl.multiple_of(slab * LANES, LANES), LANES), :] = nt(eye_ref[...], f.astype(BF16)).astype(BF16)
        chn[slab] = stacked(values)

    def near_prep(u, c):
        at = pl.ds(pl.multiple_of(u * LANES, LANES), LANES)
        x = p8[:, at]
        near_source(u + 1, rhs_ref[:, at], source_rows(x))
        bias = pltpu.roll(pltpu.roll(nlb[...], (LANES - 2 * u) % LANES, axis=1), (2 * u) % 8, axis=0)
        bias = nn(bias.astype(BF16), sel2)
        xn[u] = jnp.concatenate(
            [*target_stack(target_rows(x)), bias, jnp.zeros((8, LANES), F32)], axis=0).astype(BF16)
        return c

    lax.fori_loop(0, 32, near_prep, 0)
    for c in near_copies:
        c.wait()
    near_source(0, rn[0, 0:16, :], rn[0, 16:24, :])
    near_source(33, rn[1, 0:16, :], rn[1, 16:24, :])

    def near_unit(u, c):
        acc = jnp.zeros((32, LANES), F32)
        at = pl.multiple_of(u * LANES, LANES)
        gh, gl = gauss(nn(ytn[pl.ds(at, 3 * LANES), :], xn[u]))
        v = jnp.concatenate([chn[u], chn[u + 1], chn[u + 2]], axis=1)
        acc = nn(v, gh) + nn(v, gl)
        out_ref[:, pl.ds(at, LANES)] = folded(acc)
        return c

    lax.fori_loop(0, 16, near_unit, 0)

    for o in range(3):
        quad_copies[o].wait_send()
    for o in range(1, 4):
        frm = (seat + o) % 4
        pltpu.make_async_remote_copy(
            src_ref=sq, dst_ref=rq.at[frm], send_sem=sem_s.at[6], recv_sem=sem_r.at[6 + frm],
            device_id=(left,), device_id_type=MESH,
        ).wait_recv()
    group = iota((24, LANES), 1) >> 5
    merged = jnp.where(group == 0, rq[0], jnp.where(group == 1, rq[1], jnp.where(group == 2, rq[2], rq[3])))
    sq2 = sn
    sq2[0] = merged
    rg[quad] = merged

    def root_copy(o, slot):
        return pltpu.make_async_remote_copy(
            src_ref=sq2.at[0], dst_ref=rg.at[slot], send_sem=gs_sem.at[o], recv_sem=gr_sem.at[slot],
            device_id=(dst(o),), device_id_type=MESH,
        )

    def root_send(o, c):
        root_copy(o, quad).start()
        return c

    lax.fori_loop(1, quads, root_send, 0)

    lax.fori_loop(16, 32, near_unit, 0)

    def level_source(slab, q_class, values, rows):
        cls = (4 * q_class + (iota((32, LANES), 1) >> 5)) % 32
        hot = jnp.where(iota((32, LANES), 0) == cls, 1.0, 0.0)
        f = jnp.concatenate([*source_stack(rows), hot], axis=0)
        at = slab * LANES if isinstance(slab, int) else pl.multiple_of(slab * LANES, LANES)
        ytc[pl.ds(at, LANES), :] = nt(eye_ref[...], f.astype(BF16)).astype(BF16)
        chc[slab] = stacked(values)

    def level_prep(u, c):
        q = jnp.where(u >= 5, u - 5, jnp.where(u >= 1, u - 1, 0))
        slab = jnp.where(u >= 5, 0, jnp.where(u >= 1, 20, 28)) + 2 + q
        x = pa[pl.ds(pl.multiple_of(u * 8, 8), 8), :]
        level_source(slab, q + 2, coef3[u], source_rows(x))
        bias = pltpu.roll(pltpu.roll(clb[...], (LANES - 4 * u) % LANES, axis=1), (4 * q) % 32, axis=0)
        bias = nn(bias.astype(BF16), sel4)
        xc[u] = jnp.concatenate([*target_stack(target_rows(x)), bias], axis=0).astype(BF16)
        return c

    lax.fori_loop(0, 21, level_prep, 0)
    for c in level_copies:
        c.wait()
    for i in range(2):
        for first, k, n in ((0, 0, 16), (20, 2, 4)):
            level_source(first + i, i, rlr[0, k + i, 0:16, :], rlr[0, k + i, 16:24, :])
            level_source(first + 2 + n + i, 2 + n + i, rlr[1, k + i, 0:16, :], rlr[1, k + i, 16:24, :])
    for i, blk in ((0, r1[0]), (1, rlr[0, 4]), (3, rlr[1, 4]), (4, r1[1])):
        level_source(28 + i, i, blk[0:16], blk[16:24])

    def couple_unit(u, c):
        q = jnp.where(u >= 5, u - 5, jnp.where(u >= 1, u - 1, 0))
        slab = jnp.where(u >= 5, 0, jnp.where(u >= 1, 20, 28)) + q
        at = pl.multiple_of(slab * LANES, LANES)
        gh, gl = gauss(nn(ytc[pl.ds(at, 5 * LANES), :], xc[u]))
        v = jnp.concatenate([chc[slab + i] for i in range(5)], axis=1)
        fc[u] = folded(nn(v, gh) + nn(v, gl))
        return c

    lax.fori_loop(0, 21, couple_unit, 0)

    froot = jnp.concatenate(target_stack(target_rows(pa[21 * 8 : 22 * 8, :])), axis=0)
    troot = nt(eye_ref[0:32, :], froot.astype(BF16)).astype(BF16)

    def root_wait(o, c):
        root_copy(o, (quad + quads - o) % quads).wait_recv()
        return c

    lax.fori_loop(1, quads, root_wait, 0)

    def root_unit(u, acc):
        f = jnp.concatenate(source_stack(rg[u, 16:24, :]), axis=0)
        gh, gl = gauss(nn(troot, f.astype(BF16)) + rb[pl.ds(u, 1), :])
        return acc + nt(stacked(rg[u, 0:16, :]), jnp.concatenate([gh, gl], axis=0))

    acc = lax.fori_loop(0, quads, root_unit, jnp.zeros((32, 64), F32))
    acc = folded(acc)
    f0 = jnp.concatenate([acc, jnp.zeros((16, 64), F32)], axis=1)

    def down(f, u):
        b = stacked(f)
        fc[u] += folded(nt(b, tbh[u]) + nt(b, tbl[u]))

    down(f0, 0)
    f1 = fc[0]
    for q in range(4):
        down(f1, 1 + q)

    def far(q, c):
        down(fc[1 + q // 4], 5 + q)
        bh, bl = basis_parts(q)
        b = stacked(fc[5 + q])
        out_ref[:, pl.ds(pl.multiple_of(q * 256, 256), 256)] += folded(nn(b, bh) + nn(b, bl))
        return c

    lax.fori_loop(0, 16, far, 0)

    for c in near_copies[:0]:
        c.wait()

    def root_done(o, c):
        root_copy(o, quad).wait_send()
        return c

    lax.fori_loop(1, quads, root_done, 0)


def body(n_dev, points, rhs, leaf_basis, transfer, proxies, near_list, couple_list, root_list):
    rlist = root_list
    if n_dev < LANES:
        rlist = jnp.pad(rlist, ((0, 0), (0, LANES - n_dev)))
    quads = n_dev // 4
    scratch = [
        pltpu.VMEM((8, 4096), F32),
        pltpu.VMEM((192, LANES), F32),
        pltpu.VMEM((84 * 32, LANES), F32),
        pltpu.VMEM((21, LANES, LANES), BF16),
        pltpu.VMEM((21, LANES, LANES), BF16),
        pltpu.VMEM((LANES, LANES), BF16),
        pltpu.VMEM((LANES, 256), BF16),
        pltpu.VMEM((34 * LANES, KN), BF16),
        pltpu.VMEM((34, 32, LANES), BF16),
        pltpu.VMEM((32, KN, LANES), BF16),
        pltpu.VMEM((33 * LANES, KC), BF16),
        pltpu.VMEM((33, 32, LANES), BF16),
        pltpu.VMEM((21, KC, LANES), BF16),
        pltpu.VMEM((32, LANES), F32),
        pltpu.VMEM((8, LANES), F32),
        pltpu.VMEM((32, LANES), F32),
        pltpu.VMEM((21, 16, LANES), F32),
        pltpu.VMEM((21, 16, LANES), F32),
        pltpu.VMEM((2, 24, LANES), F32),
        pltpu.VMEM((2, 24, LANES), F32),
        pltpu.VMEM((2, 5, 24, LANES), F32),
        pltpu.VMEM((2, 5, 24, LANES), F32),
        pltpu.VMEM((24, LANES), F32),
        pltpu.VMEM((2, 24, LANES), F32),
        pltpu.VMEM((24, LANES), F32),
        pltpu.VMEM((4, 24, LANES), F32),
        pltpu.VMEM((quads, 24, LANES), F32),
        pltpu.SemaphoreType.DMA((10,)),
        pltpu.SemaphoreType.DMA((10,)),
        pltpu.SemaphoreType.DMA((quads,)),
        pltpu.SemaphoreType.DMA((quads,)),
    ]
    vmem = pl.BlockSpec(memory_space=pltpu.VMEM)
    return pl.pallas_call(
        functools.partial(kernel, n_dev),
        out_shape=jax.ShapeDtypeStruct(rhs.shape, F32),
        in_specs=[vmem] * 8,
        out_specs=vmem,
        scratch_shapes=scratch,
        compiler_params=pltpu.CompilerParams(
            collective_id=0, has_side_effects=True, vmem_limit_bytes=40 * 2**20
        ),
        name="hmatvec",
    )(points, rhs, leaf_basis, transfer, proxies, near_list.T, couple_list.T, rlist)


def solution(mesh):
    n_dev = mesh.shape["leaf"]
    in_specs = (
        P(None, "leaf"), P(None, "leaf"), P(None, "leaf"), P(None, None, "leaf"), P(None, None, "leaf"),
        P("leaf", None), P("leaf", None), P("leaf", None),
    )
    return jax.shard_map(
        functools.partial(body, n_dev), mesh=mesh, in_specs=in_specs, out_specs=P(None, "leaf"), check_vma=False
    )
```

```python
import functools
import math

import jax
import jax.numpy as jnp
from jax import lax
from jax.experimental import pallas as pl
from jax.experimental.pallas import tpu as pltpu
from jax.sharding import PartitionSpec as P

F32, BF16 = jnp.float32, jnp.bfloat16
MESH = pl.DeviceIdType.MESH
BIG = 16384.0
SCALE = math.sqrt(10.0 * math.log2(math.e))
LANES = 128
KN = 64
KC = 80


def nt(a, b):
    return lax.dot_general(a, b, (((1,), (1,)), ((), ())), preferred_element_type=F32)


def nn(a, b):
    return lax.dot_general(a, b, (((1,), (0,)), ((), ())), preferred_element_type=F32)


def iota(shape, dim):
    return lax.broadcasted_iota(jnp.int32, shape, dim)


def halves(x):
    hi = x.astype(BF16)
    return hi, (x - hi.astype(F32)).astype(BF16)


def stacked(x):
    hi = x.astype(BF16).astype(F32)
    return jnp.concatenate([hi, x - hi], axis=0).astype(BF16)


def folded(x):
    n = x.shape[0] // 2
    return x[:n] + x[n:]


def thirds(x):
    h = x.astype(BF16).astype(F32)
    m = (x - h).astype(BF16).astype(F32)
    return h, m, x - h - m


def source_rows(x):
    r = iota(x.shape, 0)
    x = jnp.where(r < 3, x, 0.0)
    n2 = jnp.sum(x * x, axis=0, keepdims=True)
    return jnp.where(r < 3, x, jnp.where(r == 3, n2, jnp.where(r == 4, 1.0, 0.0)))


def target_rows(x):
    r = iota(x.shape, 0)
    x = jnp.where(r < 3, x, 0.0)
    n2 = jnp.sum(x * x, axis=0, keepdims=True)
    return jnp.where(r < 3, 2.0 * x, jnp.where(r == 3, -1.0, jnp.where(r == 4, -n2, 0.0)))


def source_stack(rows):
    h, m, l = thirds(rows)
    return [h, m, l, h, m, h]


def target_stack(rows):
    h, m, l = thirds(rows)
    return [h, h, h, m, m, l]


def gauss(e):
    g = jnp.exp2(e)
    return halves(g)


def kernel(
    n_dev,
    pts_hbm, rhs_hbm, basis_hbm, tr_hbm, px_hbm, nl_hbm, cl_hbm, rl_hbm,
    out_ref,
    pts_ref, rhs_ref, basis_ref, tr_ref, px_ref, nl_ref, cl_ref, rl_ref, in_sem,
    nr, p8, pa, tb, tbh, tbl, eye_ref, bmask,
    ytn, chn, xn, ytc, chc, xc, xc1, clb, nlb, rb,
    gc, fc, fd,
    sn, rn, sl, rlr, s1, r1, sq, rq, rg,
    sem_s, sem_r, gs_sem, gr_sem,
):
    loads = {
        name: pltpu.make_async_copy(src, dst, in_sem.at[i])
        for i, (name, src, dst) in enumerate((
            ("tr", tr_hbm, tr_ref), ("px", px_hbm, px_ref), ("basis", basis_hbm, basis_ref),
            ("rhs", rhs_hbm, rhs_ref), ("pts", pts_hbm, pts_ref), ("nl", nl_hbm, nl_ref),
            ("cl", cl_hbm, cl_ref), ("rl", rl_hbm, rl_ref),
        ))
    }
    for c in loads.values():
        c.start()
    me = lax.axis_index("leaf")
    quads = n_dev // 4
    quad, seat = me // 4, me % 4
    left, right = (me + n_dev - 1) % n_dev, (me + 1) % n_dev
    left2, right2 = (me + n_dev - 2) % n_dev, (me + 2) % n_dev
    peers = [quad * 4 + (seat + o) % 4 for o in range(1, 4)]

    def dst(o):
        return ((quad + o) % quads) * 4 + seat

    barrier = pltpu.get_barrier_semaphore()
    for d in [left, right, left2, right2, *peers]:
        pl.semaphore_signal(barrier, inc=1, device_id=(d,), device_id_type=MESH)

    def greet(o, c):
        pl.semaphore_signal(barrier, inc=1, device_id=(dst(o),), device_id_type=MESH)
        return c

    lax.fori_loop(1, quads, greet, 0)

    eye_ref[...] = jnp.where(iota((LANES, LANES), 0) == iota((LANES, LANES), 1), 1.0, 0.0).astype(BF16)
    bmask[...] = jnp.where(iota((LANES, 256), 0) // 32 == iota((LANES, 256), 1) // 64, 1.0, 0.0).astype(BF16)

    loads["tr"].wait()
    lane_n, row_n = iota((LANES, 84), 1), iota((LANES, 84), 0)
    tmask = (lane_n < 4) | (((lane_n >> 2) + 3) % 4 == (row_n >> 5))
    eye84 = jnp.where(iota((84, 84), 0) == iota((84, 84), 1), 1.0, 0.0).astype(BF16)

    def turn(a, c):
        w = tr_ref[a]
        w = jnp.where(tmask, jnp.concatenate([w, w, w, w], axis=0), 0.0)
        hi, lo = halves(w)
        tb[pl.ds(a, 84, stride=32), :] = nt(eye84, hi) + nt(eye84, lo)
        return c

    lax.fori_loop(0, 32, turn, 0, unroll=4)

    def part(i, c):
        hi, lo = halves(tb[pl.ds(i * LANES, LANES), :])
        tbh[i] = hi
        tbl[i] = lo
        return c

    lax.fori_loop(0, 21, part, 0, unroll=3)

    loads["px"].wait()
    pick = jnp.where(
        ((iota((24, 85), 1) >= 1) & ((iota((24, 85), 1) - 1) >> 2 == iota((24, 85), 0)))
        | ((iota((24, 85), 1) == 0) & (iota((24, 85), 0) == 21)), 1.0, 0.0).astype(BF16)
    lane_p, row_p = iota((LANES, 85), 1), iota((LANES, 85), 0)
    pmask = (lane_p == 0) | ((lane_p + 3) % 4 == (row_p >> 5))
    pa[...] = jnp.zeros_like(pa)
    for ax in range(3):
        w = (px_ref[ax] - 0.5) * SCALE
        w = jnp.where(pmask, jnp.concatenate([w, w, w, w], axis=0), 0.0)
        h, m, l = thirds(w)
        pa[pl.ds(ax, 24, stride=8), :] = (
            nt(pick, h.astype(BF16)) + nt(pick, m.astype(BF16)) + nt(pick, l.astype(BF16))
        )

    def basis_parts(q):
        hi, lo = halves(basis_ref[:, pl.ds(q * 256, 256)])
        mask = bmask[...]
        return (
            jnp.concatenate([hi, hi, hi, hi], axis=0) * mask,
            jnp.concatenate([lo, lo, lo, lo], axis=0) * mask,
        )

    loads["basis"].wait()
    loads["rhs"].wait()
    coef3 = gc

    def leaf_coef(q, c):
        bh, bl = basis_parts(q)
        v = stacked(rhs_ref[:, pl.ds(q * 256, 256)])
        coef3[5 + q] = folded(nt(v, bh) + nt(v, bl))
        return c

    lax.fori_loop(0, 16, leaf_coef, 0, unroll=4)

    for r in range(4):
        acc = jnp.zeros((32, LANES), F32)
        for i in range(4):
            b = stacked(coef3[5 + 4 * r + i])
            acc += nn(b, tbh[5 + 4 * r + i]) + nn(b, tbl[5 + 4 * r + i])
        coef3[1 + r] = folded(acc)
    acc = jnp.zeros((32, LANES), F32)
    for i in range(4):
        b = stacked(coef3[1 + i])
        acc += nn(b, tbh[1 + i]) + nn(b, tbl[1 + i])
    coef3[0] = folded(acc)
    b = stacked(coef3[0])
    coef0 = folded(nn(b, tbh[0]) + nn(b, tbl[0]))

    pl.semaphore_wait(barrier, 7 + quads - 1)

    def remote(src, dst_ref, i, d):
        return pltpu.make_async_remote_copy(
            src_ref=src, dst_ref=dst_ref, send_sem=sem_s.at[i], recv_sem=sem_r.at[i],
            device_id=(d,), device_id_type=MESH,
        )

    sq[0:16, :] = coef0
    sq[16:24, :] = source_rows(pa[21 * 8 : 22 * 8, :])
    for i, (to_left, to_right) in enumerate(((5, 19), (6, 20), (1, 3), (2, 4), (0, 0))):
        for side, u in ((0, to_left), (1, to_right)):
            sl[side, i, 0:16, :] = coef3[u]
            sl[side, i, 16:24, :] = source_rows(pa[u * 8 : u * 8 + 8, :])
    s1[0:16, :] = coef3[0]
    s1[16:24, :] = source_rows(pa[0:8, :])
    rq[seat] = sq[...]
    quad_copies = [
        pltpu.make_async_remote_copy(
            src_ref=sq, dst_ref=rq.at[seat], send_sem=sem_s.at[6 + o], recv_sem=sem_r.at[6 + seat],
            device_id=(peers[o],), device_id_type=MESH,
        )
        for o in range(3)
    ]
    for c in quad_copies:
        c.start()
    level_copies = [
        remote(sl.at[0], rlr.at[1], 2, left),
        remote(sl.at[1], rlr.at[0], 3, right),
        remote(s1, r1.at[1], 4, left2),
        remote(s1, r1.at[0], 5, right2),
    ]
    for c in level_copies:
        c.start()

    loads["pts"].wait()
    p8[...] = jnp.zeros_like(p8)
    p8[0:3, :] = (pts_ref[...] - 0.5) * SCALE
    for i, u in ((0, 0), (1, 31)):
        sn[i, 0:16, :] = rhs_ref[:, u * LANES : (u + 1) * LANES]
        sn[i, 16:24, :] = source_rows(p8[:, u * LANES : (u + 1) * LANES])

    near_copies = [
        remote(sn.at[0], rn.at[1], 0, left),
        remote(sn.at[1], rn.at[0], 1, right),
    ]
    for c in near_copies:
        c.start()

    for name in ("nl", "cl", "rl"):
        loads[name].wait()

    clb[...] = jnp.full_like(clb, -BIG)
    clb[0:20, 0:84] = jnp.where(cl_ref[...] >= 0, 0.0, -BIG)
    nlb[...] = jnp.full_like(nlb, -BIG)
    nlb[0:5, 0:64] = jnp.where(nl_ref[...] >= 0, 0.0, -BIG)
    nb = nlb[...]
    h = iota((8, LANES), 1) % 4
    for k in range(1, 4):
        nb = jnp.where(h == k, pltpu.roll(nlb[...], k, axis=0), nb)
    nlb[...] = nb
    cb = clb[...]
    clb[...] = jnp.where((iota((32, LANES), 1) + 4) % 8 >= 4, pltpu.roll(cb, 4, axis=0), cb)
    c1b = cb
    sel8 = jnp.where(iota((LANES, 256), 0) == iota((LANES, 256), 1) >> 5, 1.0, 0.0).astype(BF16)
    sel4 = jnp.where(iota((LANES, 256), 0) == iota((LANES, 256), 1) >> 6, 1.0, 0.0).astype(BF16)
    selm = jnp.where(iota((LANES, LANES), 0) % 4 == iota((LANES, LANES), 1) >> 5, 1.0, 0.0).astype(BF16)
    rlist = jnp.where(rl_ref[...] >= 0, 0.0, -BIG) + jnp.zeros((32, LANES), F32)
    rlist = jnp.where(iota((32, LANES), 1) >> 2 == iota((32, LANES), 0), rlist, 0.0)
    rb[...] = nn(rlist.astype(BF16), selm)

    def near_source(slab, values, rows):
        cls = (2 * slab + (iota((8, LANES), 1) >> 6)) % 8
        hot = jnp.where(iota((8, LANES), 0) == cls, 1.0, 0.0)
        f = jnp.concatenate([*source_stack(rows), hot, jnp.zeros((8, LANES), F32)], axis=0)
        ytn[pl.ds(pl.multiple_of(slab * LANES, LANES), LANES), :] = nt(eye_ref[...], f.astype(BF16)).astype(BF16)
        chn[slab] = stacked(values)

    def near_prep(v, c):
        for i in range(2):
            at = pl.ds(pl.multiple_of((2 * v + i) * LANES, LANES), LANES)
            near_source(2 * v + i + 1, rhs_ref[:, at], source_rows(p8[:, at]))
        x = p8[:, pl.ds(pl.multiple_of(v * 256, 256), 256)]
        bias = pltpu.roll(pltpu.roll(nlb[...], (LANES - 4 * v) % LANES, axis=1), (4 * v) % 8, axis=0)
        bias = nn(bias.astype(BF16), sel4)
        xn[v] = jnp.concatenate(
            [*target_stack(target_rows(x)), bias, jnp.zeros((8, 256), F32)], axis=0).astype(BF16)
        return c

    lax.fori_loop(0, 16, near_prep, 0, unroll=4)
    for c in near_copies:
        c.wait()
    near_source(0, rn[0, 0:16, :], rn[0, 16:24, :])
    near_source(33, rn[1, 0:16, :], rn[1, 16:24, :])

    def near_unit(v, c):
        gh, gl = gauss(nn(ytn[pl.ds(pl.multiple_of(v * 256, 256), 512), :], xn[v]))
        b = jnp.concatenate([chn[2 * v + i] for i in range(4)], axis=1)
        nr[:, pl.ds(pl.multiple_of(v * 256, 256), 256)] = folded(nn(b, gh) + nn(b, gl))
        return c

    lax.fori_loop(0, 8, near_unit, 0, unroll=2)

    for o in range(3):
        quad_copies[o].wait_send()
    for o in range(1, 4):
        frm = (seat + o) % 4
        pltpu.make_async_remote_copy(
            src_ref=sq, dst_ref=rq.at[frm], send_sem=sem_s.at[6], recv_sem=sem_r.at[6 + frm],
            device_id=(left,), device_id_type=MESH,
        ).wait_recv()
    group = iota((24, LANES), 1) >> 5
    merged = jnp.where(group == 0, rq[0], jnp.where(group == 1, rq[1], jnp.where(group == 2, rq[2], rq[3])))
    sq2 = sn
    sq2[0] = merged
    rg[quad] = merged

    def root_copy(o, slot):
        return pltpu.make_async_remote_copy(
            src_ref=sq2.at[0], dst_ref=rg.at[slot], send_sem=gs_sem.at[o], recv_sem=gr_sem.at[slot],
            device_id=(dst(o),), device_id_type=MESH,
        )

    def root_send(o, c):
        root_copy(o, quad).start()
        return c

    lax.fori_loop(1, quads, root_send, 0)

    lax.fori_loop(8, 16, near_unit, 0, unroll=2)

    def level_source(slab, q_class, values, rows):
        cls = (4 * q_class + (iota((32, LANES), 1) >> 5)) % 32
        hot = jnp.where(iota((32, LANES), 0) == cls, 1.0, 0.0)
        f = jnp.concatenate([*source_stack(rows), hot], axis=0)
        at = slab * LANES if isinstance(slab, int) else pl.multiple_of(slab * LANES, LANES)
        ytc[pl.ds(at, LANES), :] = nt(eye_ref[...], f.astype(BF16)).astype(BF16)
        chc[slab] = stacked(values)

    def level_prep(w, c):
        q = jnp.where(w < 8, 2 * w, 2 * w - 16)
        u = q + jnp.where(w < 8, 5, 1)
        slab = q + jnp.where(w < 8, 2, 22)
        xs = [pa[pl.ds(pl.multiple_of((u + i) * 8, 8), 8), :] for i in range(2)]
        for i in range(2):
            level_source(slab + i, q + 2 + i, coef3[u + i], source_rows(xs[i]))
        bias = pltpu.roll(pltpu.roll(clb[...], (LANES - 4 * u) % LANES, axis=1), (4 * q) % 32, axis=0)
        bias = nn(bias.astype(BF16), sel8)
        xs = target_rows(jnp.concatenate(xs, axis=1))
        xc[w] = jnp.concatenate([*target_stack(xs), bias], axis=0).astype(BF16)
        return c

    lax.fori_loop(0, 10, level_prep, 0, unroll=2)
    level_source(30, 2, coef3[0], source_rows(pa[0:8, :]))
    bias = nn(c1b.astype(BF16), sel8[:, 0:LANES])
    xc1[...] = jnp.concatenate([*target_stack(target_rows(pa[0:8, :])), bias], axis=0).astype(BF16)
    for c in level_copies:
        c.wait()
    for i in range(2):
        for first, k, n in ((0, 0, 16), (20, 2, 4)):
            level_source(first + i, i, rlr[0, k + i, 0:16, :], rlr[0, k + i, 16:24, :])
            level_source(first + 2 + n + i, 2 + n + i, rlr[1, k + i, 0:16, :], rlr[1, k + i, 16:24, :])
    for i, blk in ((0, r1[0]), (1, rlr[0, 4]), (3, rlr[1, 4]), (4, r1[1])):
        level_source(28 + i, i, blk[0:16], blk[16:24])

    def couple_unit(w, c):
        q = jnp.where(w < 8, 2 * w, 2 * w - 16)
        u = q + jnp.where(w < 8, 5, 1)
        slab = q + jnp.where(w < 8, 0, 20)
        gh, gl = gauss(nn(ytc[pl.ds(pl.multiple_of(slab * LANES, LANES), 6 * LANES), :], xc[w]))
        b = jnp.concatenate([chc[slab + i] for i in range(6)], axis=1)
        g = folded(nn(b, gh) + nn(b, gl))
        fc[u] = g[:, 0:LANES]
        fc[u + 1] = g[:, LANES:256]
        return c

    lax.fori_loop(0, 10, couple_unit, 0, unroll=2)
    gh, gl = gauss(nn(ytc[28 * LANES : 33 * LANES, :], xc1[...]))
    b = jnp.concatenate([chc[28 + i] for i in range(5)], axis=1)
    fc[0] = folded(nn(b, gh) + nn(b, gl))

    froot = jnp.concatenate(target_stack(target_rows(pa[21 * 8 : 22 * 8, :])), axis=0)
    troot = nt(eye_ref[0:32, :], froot.astype(BF16)).astype(BF16)

    def root_wait(o, c):
        root_copy(o, (quad + quads - o) % quads).wait_recv()
        return c

    lax.fori_loop(1, quads, root_wait, 0)

    def root_unit(u, acc):
        f = jnp.concatenate(source_stack(rg[u, 16:24, :]), axis=0)
        gh, gl = gauss(nn(troot, f.astype(BF16)) + rb[pl.ds(u, 1), :])
        return acc + nt(stacked(rg[u, 0:16, :]), jnp.concatenate([gh, gl], axis=0))

    acc = lax.fori_loop(0, quads, root_unit, jnp.zeros((32, 64), F32), unroll=min(4, quads))
    acc = folded(acc)
    f0 = jnp.concatenate([acc, jnp.zeros((16, 64), F32)], axis=1)

    def down(f, u):
        b = stacked(f)
        return fc[u] + folded(nt(b, tbh[u]) + nt(b, tbl[u]))

    f1 = down(f0, 0)
    for q in range(4):
        fd[q] = down(f1, 1 + q)

    def far(q, c):
        at = pl.ds(pl.multiple_of(q * 256, 256), 256)
        bh, bl = basis_parts(q)
        b = stacked(down(fd[q // 4], 5 + q))
        out_ref[:, at] = nr[:, at] + folded(nn(b, bh) + nn(b, bl))
        return c

    lax.fori_loop(0, 16, far, 0, unroll=4)

    def root_done(o, c):
        root_copy(o, quad).wait_send()
        return c

    lax.fori_loop(1, quads, root_done, 0)


def body(n_dev, points, rhs, leaf_basis, transfer, proxies, near_list, couple_list, root_list):
    rlist = root_list
    if n_dev < LANES:
        rlist = jnp.pad(rlist, ((0, 0), (0, LANES - n_dev)))
    quads = n_dev // 4
    ins = [(3, 4096), (16, 4096), (32, 4096), (32, 32, 84), (3, 32, 85), (5, 64), (20, 84), (1, LANES)]
    scratch = [
        *[pltpu.VMEM(shape, F32 if i < 5 else jnp.int32) for i, shape in enumerate(ins)],
        pltpu.SemaphoreType.DMA((8,)),
        pltpu.VMEM((16, 4096), F32),
        pltpu.VMEM((8, 4096), F32),
        pltpu.VMEM((192, LANES), F32),
        pltpu.VMEM((84 * 32, LANES), F32),
        pltpu.VMEM((21, LANES, LANES), BF16),
        pltpu.VMEM((21, LANES, LANES), BF16),
        pltpu.VMEM((LANES, LANES), BF16),
        pltpu.VMEM((LANES, 256), BF16),
        pltpu.VMEM((34 * LANES, KN), BF16),
        pltpu.VMEM((34, 32, LANES), BF16),
        pltpu.VMEM((16, KN, 256), BF16),
        pltpu.VMEM((33 * LANES, KC), BF16),
        pltpu.VMEM((33, 32, LANES), BF16),
        pltpu.VMEM((10, KC, 256), BF16),
        pltpu.VMEM((KC, LANES), BF16),
        pltpu.VMEM((32, LANES), F32),
        pltpu.VMEM((8, LANES), F32),
        pltpu.VMEM((32, LANES), F32),
        pltpu.VMEM((21, 16, LANES), F32),
        pltpu.VMEM((21, 16, LANES), F32),
        pltpu.VMEM((4, 16, LANES), F32),
        pltpu.VMEM((2, 24, LANES), F32),
        pltpu.VMEM((2, 24, LANES), F32),
        pltpu.VMEM((2, 5, 24, LANES), F32),
        pltpu.VMEM((2, 5, 24, LANES), F32),
        pltpu.VMEM((24, LANES), F32),
        pltpu.VMEM((2, 24, LANES), F32),
        pltpu.VMEM((24, LANES), F32),
        pltpu.VMEM((4, 24, LANES), F32),
        pltpu.VMEM((quads, 24, LANES), F32),
        pltpu.SemaphoreType.DMA((10,)),
        pltpu.SemaphoreType.DMA((10,)),
        pltpu.SemaphoreType.DMA((quads,)),
        pltpu.SemaphoreType.DMA((quads,)),
    ]
    vmem = pl.BlockSpec(memory_space=pltpu.VMEM)
    return pl.pallas_call(
        functools.partial(kernel, n_dev),
        out_shape=jax.ShapeDtypeStruct(rhs.shape, F32),
        in_specs=[pl.BlockSpec(memory_space=pltpu.HBM)] * 8,
        out_specs=vmem,
        scratch_shapes=scratch,
        compiler_params=pltpu.CompilerParams(
            collective_id=0, has_side_effects=True, vmem_limit_bytes=40 * 2**20
        ),
        name="hmatvec",
    )(points, rhs, leaf_basis, transfer, proxies, near_list.T, couple_list.T, rlist)


def solution(mesh):
    n_dev = mesh.shape["leaf"]
    in_specs = (
        P(None, "leaf"), P(None, "leaf"), P(None, "leaf"), P(None, None, "leaf"), P(None, None, "leaf"),
        P("leaf", None), P("leaf", None), P("leaf", None),
    )
    return jax.shard_map(
        functools.partial(body, n_dev), mesh=mesh, in_specs=in_specs, out_specs=P(None, "leaf"), check_vma=False
    )
```

```python
import functools
import math

import jax
import jax.numpy as jnp
from jax import lax
from jax.experimental import pallas as pl
from jax.experimental.pallas import tpu as pltpu
from jax.sharding import PartitionSpec as P

F32, BF16 = jnp.float32, jnp.bfloat16
MESH = pl.DeviceIdType.MESH
BIG = 16384.0
SCALE = math.sqrt(10.0 * math.log2(math.e))
LANES = 128
KN = 64
KC = 80


def nt(a, b):
    return lax.dot_general(a, b, (((1,), (1,)), ((), ())), preferred_element_type=F32)


def nn(a, b):
    return lax.dot_general(a, b, (((1,), (0,)), ((), ())), preferred_element_type=F32)


def iota(shape, dim):
    return lax.broadcasted_iota(jnp.int32, shape, dim)


def halves(x):
    hi = x.astype(BF16)
    return hi, (x - hi.astype(F32)).astype(BF16)


def stacked(x):
    hi = x.astype(BF16).astype(F32)
    return jnp.concatenate([hi, x - hi], axis=0).astype(BF16)


def folded(x):
    n = x.shape[0] // 2
    return x[:n] + x[n:]


def thirds(x):
    h = x.astype(BF16).astype(F32)
    m = (x - h).astype(BF16).astype(F32)
    return h, m, x - h - m


def source_rows(x):
    r = iota(x.shape, 0)
    x = jnp.where(r < 3, x, 0.0)
    n2 = jnp.sum(x * x, axis=0, keepdims=True)
    return jnp.where(r < 3, x, jnp.where(r == 3, n2, jnp.where(r == 4, 1.0, 0.0)))


def target_rows(x):
    r = iota(x.shape, 0)
    x = jnp.where(r < 3, x, 0.0)
    n2 = jnp.sum(x * x, axis=0, keepdims=True)
    return jnp.where(r < 3, 2.0 * x, jnp.where(r == 3, -1.0, jnp.where(r == 4, -n2, 0.0)))


def source_stack(rows):
    h, m, l = thirds(rows)
    return [h, m, l, h, m, h]


def target_stack(rows):
    h, m, l = thirds(rows)
    return [h, h, h, m, m, l]


def once(fn):
    fn()


def gauss(e):
    g = jnp.exp2(e)
    return halves(g)


def kernel(
    n_dev,
    pts_hbm, rhs_hbm, basis_hbm, tr_hbm, px_hbm, nl_hbm, cl_hbm, rl_hbm,
    out_ref,
    pts_ref, rhs_ref, basis_ref, tr_ref, px_ref, nl_ref, cl_ref, rl_ref, in_sem,
    nr, p8, pa, tb, tbh, tbl, eye_ref, bmask,
    ytn, chn, xn, ytc, chc, xc, xc1, clb, nlb, rb,
    gc, fc, fd,
    sn, rn, sl, rlr, s1, r1, sq, sq2, rq, rg,
    sem_s, sem_r, gs_sem, gr_sem,
):
    loads = {
        name: pltpu.make_async_copy(src, dst, in_sem.at[i])
        for i, (name, src, dst) in enumerate((
            ("tr", tr_hbm, tr_ref), ("px", px_hbm, px_ref), ("basis", basis_hbm, basis_ref),
            ("rhs", rhs_hbm, rhs_ref), ("pts", pts_hbm, pts_ref), ("nl", nl_hbm, nl_ref),
            ("cl", cl_hbm, cl_ref), ("rl", rl_hbm, rl_ref),
        ))
    }
    for c in loads.values():
        c.start()
    me = lax.axis_index("leaf")
    quads = n_dev // 4
    quad, seat = me // 4, me % 4
    left, right = (me + n_dev - 1) % n_dev, (me + 1) % n_dev
    left2, right2 = (me + n_dev - 2) % n_dev, (me + 2) % n_dev
    peers = [quad * 4 + (seat + o) % 4 for o in range(1, 4)]

    def dst(o):
        return ((quad + o) % quads) * 4 + seat

    barrier = pltpu.get_barrier_semaphore()
    for d in [left, right, left2, right2, *peers]:
        pl.semaphore_signal(barrier, inc=1, device_id=(d,), device_id_type=MESH)

    def greet(o, c):
        pl.semaphore_signal(barrier, inc=1, device_id=(dst(o),), device_id_type=MESH)
        return c

    lax.fori_loop(1, quads, greet, 0)

    def sec_const():
        eye_ref[...] = jnp.where(iota((LANES, LANES), 0) == iota((LANES, LANES), 1), 1.0, 0.0).astype(BF16)
        bmask[...] = jnp.where(iota((LANES, 256), 0) // 32 == iota((LANES, 256), 1) // 64, 1.0, 0.0).astype(BF16)

    once(sec_const)

    loads["tr"].wait()
    lane_n, row_n = iota((LANES, 84), 1), iota((LANES, 84), 0)
    tmask = (lane_n < 4) | (((lane_n >> 2) + 3) % 4 == (row_n >> 5))
    eye84 = jnp.where(iota((84, 84), 0) == iota((84, 84), 1), 1.0, 0.0).astype(BF16)

    def turn(a, c):
        w = tr_ref[a]
        w = jnp.where(tmask, jnp.concatenate([w, w, w, w], axis=0), 0.0)
        hi, lo = halves(w)
        tb[pl.ds(a, 84, stride=32), :] = nt(eye84, hi) + nt(eye84, lo)
        return c

    lax.fori_loop(0, 32, turn, 0, unroll=4)

    def part(i, c):
        hi, lo = halves(tb[pl.ds(i * LANES, LANES), :])
        tbh[i] = hi
        tbl[i] = lo
        return c

    lax.fori_loop(0, 21, part, 0, unroll=3)

    loads["px"].wait()
    def sec_prox():
        pick = jnp.where(
            ((iota((24, 85), 1) >= 1) & ((iota((24, 85), 1) - 1) >> 2 == iota((24, 85), 0)))
            | ((iota((24, 85), 1) == 0) & (iota((24, 85), 0) == 21)), 1.0, 0.0).astype(BF16)
        lane_p, row_p = iota((LANES, 85), 1), iota((LANES, 85), 0)
        pmask = (lane_p == 0) | ((lane_p + 3) % 4 == (row_p >> 5))
        pa[...] = jnp.zeros_like(pa)
        for ax in range(3):
            w = (px_ref[ax] - 0.5) * SCALE
            w = jnp.where(pmask, jnp.concatenate([w, w, w, w], axis=0), 0.0)
            h, m, l = thirds(w)
            pa[pl.ds(ax, 24, stride=8), :] = (
                nt(pick, h.astype(BF16)) + nt(pick, m.astype(BF16)) + nt(pick, l.astype(BF16))
            )

    once(sec_prox)

    def basis_parts(q):
        hi, lo = halves(basis_ref[:, pl.ds(q * 256, 256)])
        mask = bmask[...]
        return (
            jnp.concatenate([hi, hi, hi, hi], axis=0) * mask,
            jnp.concatenate([lo, lo, lo, lo], axis=0) * mask,
        )

    loads["basis"].wait()
    loads["rhs"].wait()
    coef3 = gc

    def leaf_coef(q, c):
        bh, bl = basis_parts(q)
        v = stacked(rhs_ref[:, pl.ds(q * 256, 256)])
        coef3[5 + q] = folded(nt(v, bh) + nt(v, bl))
        return c

    lax.fori_loop(0, 16, leaf_coef, 0, unroll=4)

    def sec_up():
        for r in range(4):
            acc = jnp.zeros((32, LANES), F32)
            for i in range(4):
                b = stacked(coef3[5 + 4 * r + i])
                acc += nn(b, tbh[5 + 4 * r + i]) + nn(b, tbl[5 + 4 * r + i])
            coef3[1 + r] = folded(acc)
        acc = jnp.zeros((32, LANES), F32)
        for i in range(4):
            b = stacked(coef3[1 + i])
            acc += nn(b, tbh[1 + i]) + nn(b, tbl[1 + i])
        coef3[0] = folded(acc)
        b = stacked(coef3[0])
        sq[0:16, :] = folded(nn(b, tbh[0]) + nn(b, tbl[0]))

    once(sec_up)

    pl.semaphore_wait(barrier, 7 + quads - 1)

    def remote(src, dst_ref, i, d):
        return pltpu.make_async_remote_copy(
            src_ref=src, dst_ref=dst_ref, send_sem=sem_s.at[i], recv_sem=sem_r.at[i],
            device_id=(d,), device_id_type=MESH,
        )

    def sec_pack():
        sq[16:24, :] = source_rows(pa[21 * 8 : 22 * 8, :])
        for i, (to_left, to_right) in enumerate(((5, 19), (6, 20), (1, 3), (2, 4), (0, 0))):
            for side, u in ((0, to_left), (1, to_right)):
                sl[side, i, 0:16, :] = coef3[u]
                sl[side, i, 16:24, :] = source_rows(pa[u * 8 : u * 8 + 8, :])
        s1[0:16, :] = coef3[0]
        s1[16:24, :] = source_rows(pa[0:8, :])

    once(sec_pack)

    rq[seat] = sq[...]
    quad_copies = [
        pltpu.make_async_remote_copy(
            src_ref=sq, dst_ref=rq.at[seat], send_sem=sem_s.at[6 + o], recv_sem=sem_r.at[6 + seat],
            device_id=(peers[o],), device_id_type=MESH,
        )
        for o in range(3)
    ]
    for c in quad_copies:
        c.start()
    level_copies = [
        remote(sl.at[0], rlr.at[1], 2, left),
        remote(sl.at[1], rlr.at[0], 3, right),
        remote(s1, r1.at[1], 4, left2),
        remote(s1, r1.at[0], 5, right2),
    ]
    for c in level_copies:
        c.start()

    loads["pts"].wait()
    p8[...] = jnp.zeros_like(p8)
    p8[0:3, :] = (pts_ref[...] - 0.5) * SCALE
    for i, u in ((0, 0), (1, 31)):
        sn[i, 0:16, :] = rhs_ref[:, u * LANES : (u + 1) * LANES]
        sn[i, 16:24, :] = source_rows(p8[:, u * LANES : (u + 1) * LANES])

    near_copies = [
        remote(sn.at[0], rn.at[1], 0, left),
        remote(sn.at[1], rn.at[0], 1, right),
    ]
    for c in near_copies:
        c.start()

    for name in ("nl", "cl", "rl"):
        loads[name].wait()

    clb[...] = jnp.full_like(clb, -BIG)
    clb[0:20, 0:84] = jnp.where(cl_ref[...] >= 0, 0.0, -BIG)
    nlb[...] = jnp.full_like(nlb, -BIG)
    nlb[0:5, 0:64] = jnp.where(nl_ref[...] >= 0, 0.0, -BIG)
    nb = nlb[...]
    h = iota((8, LANES), 1) % 4
    for k in range(1, 4):
        nb = jnp.where(h == k, pltpu.roll(nlb[...], k, axis=0), nb)
    nlb[...] = nb
    cb = clb[...]
    clb[...] = jnp.where((iota((32, LANES), 1) + 4) % 8 >= 4, pltpu.roll(cb, 4, axis=0), cb)
    c1b = cb
    sel8 = jnp.where(iota((LANES, 256), 0) == iota((LANES, 256), 1) >> 5, 1.0, 0.0).astype(BF16)
    sel4 = jnp.where(iota((LANES, 256), 0) == iota((LANES, 256), 1) >> 6, 1.0, 0.0).astype(BF16)
    selm = jnp.where(iota((LANES, LANES), 0) % 4 == iota((LANES, LANES), 1) >> 5, 1.0, 0.0).astype(BF16)
    rlist = jnp.where(rl_ref[...] >= 0, 0.0, -BIG) + jnp.zeros((32, LANES), F32)
    rlist = jnp.where(iota((32, LANES), 1) >> 2 == iota((32, LANES), 0), rlist, 0.0)
    rb[...] = nn(rlist.astype(BF16), selm)

    def near_source(slab, values, rows):
        cls = (2 * slab + (iota((8, LANES), 1) >> 6)) % 8
        hot = jnp.where(iota((8, LANES), 0) == cls, 1.0, 0.0)
        f = jnp.concatenate([*source_stack(rows), hot, jnp.zeros((8, LANES), F32)], axis=0)
        ytn[pl.ds(pl.multiple_of(slab * LANES, LANES), LANES), :] = nt(eye_ref[...], f.astype(BF16)).astype(BF16)
        chn[slab] = stacked(values)

    def near_prep(v, c):
        for i in range(2):
            at = pl.ds(pl.multiple_of((2 * v + i) * LANES, LANES), LANES)
            near_source(2 * v + i + 1, rhs_ref[:, at], source_rows(p8[:, at]))
        x = p8[:, pl.ds(pl.multiple_of(v * 256, 256), 256)]
        bias = pltpu.roll(pltpu.roll(nlb[...], (LANES - 4 * v) % LANES, axis=1), (4 * v) % 8, axis=0)
        bias = nn(bias.astype(BF16), sel4)
        xn[v] = jnp.concatenate(
            [*target_stack(target_rows(x)), bias, jnp.zeros((8, 256), F32)], axis=0).astype(BF16)
        return c

    lax.fori_loop(0, 16, near_prep, 0, unroll=4)

    def near_unit(v, c):
        gh, gl = gauss(nn(ytn[pl.ds(pl.multiple_of(v * 256, 256), 512), :], xn[v]))
        b = jnp.concatenate([chn[2 * v + i] for i in range(4)], axis=1)
        nr[:, pl.ds(pl.multiple_of(v * 256, 256), 256)] = folded(nn(b, gh) + nn(b, gl))
        return c

    lax.fori_loop(1, 7, near_unit, 0, unroll=2)

    for o in range(3):
        quad_copies[o].wait_send()
    for o in range(1, 4):
        frm = (seat + o) % 4
        pltpu.make_async_remote_copy(
            src_ref=sq, dst_ref=rq.at[frm], send_sem=sem_s.at[6], recv_sem=sem_r.at[6 + frm],
            device_id=(left,), device_id_type=MESH,
        ).wait_recv()
    group = iota((24, LANES), 1) >> 5
    merged = jnp.where(group == 0, rq[0], jnp.where(group == 1, rq[1], jnp.where(group == 2, rq[2], rq[3])))
    sq2[...] = merged
    rg[quad] = merged

    def root_copy(o, slot):
        return pltpu.make_async_remote_copy(
            src_ref=sq2, dst_ref=rg.at[slot], send_sem=gs_sem.at[o], recv_sem=gr_sem.at[slot],
            device_id=(dst(o),), device_id_type=MESH,
        )

    def root_send(o, c):
        root_copy(o, quad).start()
        return c

    lax.fori_loop(1, quads, root_send, 0)

    lax.fori_loop(7, 15, near_unit, 0, unroll=2)

    def level_source(slab, q_class, values, rows):
        cls = (4 * q_class + (iota((32, LANES), 1) >> 5)) % 32
        hot = jnp.where(iota((32, LANES), 0) == cls, 1.0, 0.0)
        f = jnp.concatenate([*source_stack(rows), hot], axis=0)
        at = slab * LANES if isinstance(slab, int) else pl.multiple_of(slab * LANES, LANES)
        ytc[pl.ds(at, LANES), :] = nt(eye_ref[...], f.astype(BF16)).astype(BF16)
        chc[slab] = stacked(values)

    def level_prep(w, c):
        q = jnp.where(w < 8, 2 * w, 2 * w - 16)
        u = q + jnp.where(w < 8, 5, 1)
        slab = q + jnp.where(w < 8, 2, 22)
        xs = [pa[pl.ds(pl.multiple_of((u + i) * 8, 8), 8), :] for i in range(2)]
        for i in range(2):
            level_source(slab + i, q + 2 + i, coef3[u + i], source_rows(xs[i]))
        bias = pltpu.roll(pltpu.roll(clb[...], (LANES - 4 * u) % LANES, axis=1), (4 * q) % 32, axis=0)
        bias = nn(bias.astype(BF16), sel8)
        xs = target_rows(jnp.concatenate(xs, axis=1))
        xc[w] = jnp.concatenate([*target_stack(xs), bias], axis=0).astype(BF16)
        return c

    lax.fori_loop(0, 10, level_prep, 0, unroll=2)
    level_source(30, 2, coef3[0], source_rows(pa[0:8, :]))
    bias = nn(c1b.astype(BF16), sel8[:, 0:LANES])
    xc1[...] = jnp.concatenate([*target_stack(target_rows(pa[0:8, :])), bias], axis=0).astype(BF16)
    for c in level_copies:
        c.wait()
    def sec_halo():
        for i in range(2):
            for first, k, n in ((0, 0, 16), (20, 2, 4)):
                level_source(first + i, i, rlr[0, k + i, 0:16, :], rlr[0, k + i, 16:24, :])
                level_source(first + 2 + n + i, 2 + n + i, rlr[1, k + i, 0:16, :], rlr[1, k + i, 16:24, :])
        for i, blk in ((0, r1[0]), (1, rlr[0, 4]), (3, rlr[1, 4]), (4, r1[1])):
            level_source(28 + i, i, blk[0:16], blk[16:24])

    once(sec_halo)

    def couple_unit(w, c):
        q = jnp.where(w < 8, 2 * w, 2 * w - 16)
        u = q + jnp.where(w < 8, 5, 1)
        slab = q + jnp.where(w < 8, 0, 20)
        gh, gl = gauss(nn(ytc[pl.ds(pl.multiple_of(slab * LANES, LANES), 6 * LANES), :], xc[w]))
        b = jnp.concatenate([chc[slab + i] for i in range(6)], axis=1)
        g = folded(nn(b, gh) + nn(b, gl))
        fc[u] = g[:, 0:LANES]
        fc[u + 1] = g[:, LANES:256]
        return c

    lax.fori_loop(0, 10, couple_unit, 0, unroll=2)
    def sec_l1():
        gh, gl = gauss(nn(ytc[28 * LANES : 33 * LANES, :], xc1[...]))
        b = jnp.concatenate([chc[28 + i] for i in range(5)], axis=1)
        fc[0] = folded(nn(b, gh) + nn(b, gl))

    once(sec_l1)

    for c in near_copies:
        c.wait()
    near_source(0, rn[0, 0:16, :], rn[0, 16:24, :])
    near_source(33, rn[1, 0:16, :], rn[1, 16:24, :])

    near_unit(0, 0)
    near_unit(15, 0)

    froot = jnp.concatenate(target_stack(target_rows(pa[21 * 8 : 22 * 8, :])), axis=0)
    troot = nt(eye_ref[0:32, :], froot.astype(BF16)).astype(BF16)

    def root_wait(o, c):
        root_copy(o, (quad + quads - o) % quads).wait_recv()
        return c

    lax.fori_loop(1, quads, root_wait, 0)

    def sec_tail():
        batch = min(8, quads)

        def root_unit(i, acc):
            us = [i * batch + j for j in range(batch)]
            rows = jnp.concatenate([rg[u, 16:24, :] for u in us], axis=1)
            f = jnp.concatenate(source_stack(rows), axis=0).astype(BF16)
            bias = jnp.concatenate([rb[pl.ds(u, 1), :] for u in us], axis=1)
            gh, gl = gauss(nn(troot, f) + bias)
            v = stacked(jnp.concatenate([rg[u, 0:16, :] for u in us], axis=1))
            return acc + nt(v, jnp.concatenate([gh, gl], axis=0))

        acc = jnp.zeros((32, 64), F32)
        for i in range(quads // batch):
            acc = root_unit(i, acc)
        acc = folded(acc)
        f0 = jnp.concatenate([acc, jnp.zeros((16, 64), F32)], axis=1)

        def down(f, u):
            b = stacked(f)
            return fc[u] + folded(nt(b, tbh[u]) + nt(b, tbl[u]))

        f1 = stacked(down(f0, 0))
        w = [t[1:5].reshape(512, LANES) for t in (tbh, tbl)]
        f2 = folded(nt(f1, w[0]) + nt(f1, w[1]))
        for r in range(4):
            b = stacked(fc[1 + r] + f2[:, r * LANES : (r + 1) * LANES])
            w = [t[5 + 4 * r : 9 + 4 * r].reshape(512, LANES) for t in (tbh, tbl)]
            f3 = folded(nt(b, w[0]) + nt(b, w[1]))
            for i in range(4):
                fd[4 * r + i] = stacked(fc[5 + 4 * r + i] + f3[:, i * LANES : (i + 1) * LANES])

    once(sec_tail)

    def far(q, c):
        at = pl.ds(pl.multiple_of(q * 256, 256), 256)
        bh, bl = basis_parts(q)
        b = fd[q]
        out_ref[:, at] = nr[:, at] + folded(nn(b, bh) + nn(b, bl))
        return c

    lax.fori_loop(0, 16, far, 0, unroll=8)

    def root_done(o, c):
        root_copy(o, quad).wait_send()
        return c

    lax.fori_loop(1, quads, root_done, 0)


def body(n_dev, points, rhs, leaf_basis, transfer, proxies, near_list, couple_list, root_list):
    rlist = root_list
    if n_dev < LANES:
        rlist = jnp.pad(rlist, ((0, 0), (0, LANES - n_dev)))
    quads = n_dev // 4
    ins = [(3, 4096), (16, 4096), (32, 4096), (32, 32, 84), (3, 32, 85), (5, 64), (20, 84), (1, LANES)]
    scratch = [
        *[pltpu.VMEM(shape, F32 if i < 5 else jnp.int32) for i, shape in enumerate(ins)],
        pltpu.SemaphoreType.DMA((8,)),
        pltpu.VMEM((16, 4096), F32),
        pltpu.VMEM((8, 4096), F32),
        pltpu.VMEM((192, LANES), F32),
        pltpu.VMEM((84 * 32, LANES), F32),
        pltpu.VMEM((21, LANES, LANES), BF16),
        pltpu.VMEM((21, LANES, LANES), BF16),
        pltpu.VMEM((LANES, LANES), BF16),
        pltpu.VMEM((LANES, 256), BF16),
        pltpu.VMEM((34 * LANES, KN), BF16),
        pltpu.VMEM((34, 32, LANES), BF16),
        pltpu.VMEM((16, KN, 256), BF16),
        pltpu.VMEM((33 * LANES, KC), BF16),
        pltpu.VMEM((33, 32, LANES), BF16),
        pltpu.VMEM((10, KC, 256), BF16),
        pltpu.VMEM((KC, LANES), BF16),
        pltpu.VMEM((32, LANES), F32),
        pltpu.VMEM((8, LANES), F32),
        pltpu.VMEM((32, LANES), F32),
        pltpu.VMEM((21, 16, LANES), F32),
        pltpu.VMEM((21, 16, LANES), F32),
        pltpu.VMEM((16, 32, LANES), BF16),
        pltpu.VMEM((2, 24, LANES), F32),
        pltpu.VMEM((2, 24, LANES), F32),
        pltpu.VMEM((2, 5, 24, LANES), F32),
        pltpu.VMEM((2, 5, 24, LANES), F32),
        pltpu.VMEM((24, LANES), F32),
        pltpu.VMEM((2, 24, LANES), F32),
        pltpu.VMEM((24, LANES), F32),
        pltpu.VMEM((24, LANES), F32),
        pltpu.VMEM((4, 24, LANES), F32),
        pltpu.VMEM((quads, 24, LANES), F32),
        pltpu.SemaphoreType.DMA((10,)),
        pltpu.SemaphoreType.DMA((10,)),
        pltpu.SemaphoreType.DMA((quads,)),
        pltpu.SemaphoreType.DMA((quads,)),
    ]
    vmem = pl.BlockSpec(memory_space=pltpu.VMEM)
    return pl.pallas_call(
        functools.partial(kernel, n_dev),
        out_shape=jax.ShapeDtypeStruct(rhs.shape, F32),
        in_specs=[pl.BlockSpec(memory_space=pltpu.HBM)] * 8,
        out_specs=vmem,
        scratch_shapes=scratch,
        compiler_params=pltpu.CompilerParams(
            collective_id=0, has_side_effects=True, vmem_limit_bytes=60 * 2**20
        ),
        name="hmatvec",
    )(points, rhs, leaf_basis, transfer, proxies, near_list.T, couple_list.T, rlist)


def solution(mesh):
    n_dev = mesh.shape["leaf"]
    in_specs = (
        P(None, "leaf"), P(None, "leaf"), P(None, "leaf"), P(None, None, "leaf"), P(None, None, "leaf"),
        P("leaf", None), P("leaf", None), P("leaf", None),
    )
    return jax.shard_map(
        functools.partial(body, n_dev), mesh=mesh, in_specs=in_specs, out_specs=P(None, "leaf"), check_vma=False
    )
```

```python
import functools
import math

import jax
import jax.numpy as jnp
from jax import lax
from jax.experimental import pallas as pl
from jax.experimental.pallas import tpu as pltpu
from jax.sharding import PartitionSpec as P

F32, BF16 = jnp.float32, jnp.bfloat16
MESH = pl.DeviceIdType.MESH
BIG = 16384.0
SCALE = math.sqrt(10.0 * math.log2(math.e))
LANES = 128
KN = 64
KC = 80


def nt(a, b):
    return lax.dot_general(a, b, (((1,), (1,)), ((), ())), preferred_element_type=F32)


def nn(a, b):
    return lax.dot_general(a, b, (((1,), (0,)), ((), ())), preferred_element_type=F32)


def iota(shape, dim):
    return lax.broadcasted_iota(jnp.int32, shape, dim)


def halves(x):
    hi = x.astype(BF16)
    return hi, (x - hi.astype(F32)).astype(BF16)


def stacked(x):
    hi = x.astype(BF16).astype(F32)
    return jnp.concatenate([hi, x - hi], axis=0).astype(BF16)


def folded(x):
    n = x.shape[0] // 2
    return x[:n] + x[n:]


def thirds(x):
    h = x.astype(BF16).astype(F32)
    m = (x - h).astype(BF16).astype(F32)
    return h, m, x - h - m


def source_rows(x):
    r = iota(x.shape, 0)
    x = jnp.where(r < 3, x, 0.0)
    n2 = jnp.sum(x * x, axis=0, keepdims=True)
    return jnp.where(r < 3, x, jnp.where(r == 3, n2, jnp.where(r == 4, 1.0, 0.0)))


def target_rows(x):
    r = iota(x.shape, 0)
    x = jnp.where(r < 3, x, 0.0)
    n2 = jnp.sum(x * x, axis=0, keepdims=True)
    return jnp.where(r < 3, 2.0 * x, jnp.where(r == 3, -1.0, jnp.where(r == 4, -n2, 0.0)))


def source_stack(rows):
    h, m, l = thirds(rows)
    return [h, m, l, h, m, h]


def target_stack(rows):
    h, m, l = thirds(rows)
    return [h, h, h, m, m, l]


def once(fn):
    fn()


def gauss(e):
    g = jnp.exp2(e)
    return halves(g)


def kernel(
    n_dev,
    pts_hbm, rhs_hbm, basis_hbm, tr_hbm, px_hbm, nl_hbm, cl_hbm, rl_hbm,
    out_ref,
    pts_ref, rhs_ref, basis_ref, tr_ref, px_ref, nl_ref, cl_ref, rl_ref, in_sem,
    nr, p8, pa, tb, tbh, tbl, eye_ref, bmask,
    ytn, chn, xn, ytc, chc, xc, xc1, clb, nlb, rb,
    gc, fc, fd,
    sn, rn, sl, rlr, s1, r1, sq, sq2, rq, rg,
    sem_s, sem_r, gs_sem, gr_sem,
):
    loads = {
        name: pltpu.make_async_copy(src, dst, in_sem.at[i])
        for i, (name, src, dst) in enumerate((
            ("px", px_hbm, px_ref), ("basis", basis_hbm, basis_ref), ("rhs", rhs_hbm, rhs_ref),
            ("tr", tr_hbm, tr_ref), ("pts", pts_hbm, pts_ref), ("nl", nl_hbm, nl_ref),
            ("cl", cl_hbm, cl_ref), ("rl", rl_hbm, rl_ref),
        ))
    }
    for c in loads.values():
        c.start()
    me = lax.axis_index("leaf")
    quads = n_dev // 4
    quad, seat = me // 4, me % 4
    left, right = (me + n_dev - 1) % n_dev, (me + 1) % n_dev
    left2, right2 = (me + n_dev - 2) % n_dev, (me + 2) % n_dev
    peers = [quad * 4 + (seat + o) % 4 for o in range(1, 4)]

    def dst(o):
        return ((quad + o) % quads) * 4 + seat

    barrier = pltpu.get_barrier_semaphore()
    for d in [left, right, left2, right2, *peers]:
        pl.semaphore_signal(barrier, inc=1, device_id=(d,), device_id_type=MESH)

    def greet(o, c):
        pl.semaphore_signal(barrier, inc=1, device_id=(dst(o),), device_id_type=MESH)
        return c

    lax.fori_loop(1, quads, greet, 0)

    def sec_const():
        eye_ref[...] = jnp.where(iota((LANES, LANES), 0) == iota((LANES, LANES), 1), 1.0, 0.0).astype(BF16)
        bmask[...] = jnp.where(iota((LANES, 256), 0) // 32 == iota((LANES, 256), 1) // 64, 1.0, 0.0).astype(BF16)

    once(sec_const)

    loads["px"].wait()
    def sec_prox():
        pick = jnp.where(
            ((iota((24, 85), 1) >= 1) & ((iota((24, 85), 1) - 1) >> 2 == iota((24, 85), 0)))
            | ((iota((24, 85), 1) == 0) & (iota((24, 85), 0) == 21)), 1.0, 0.0).astype(BF16)
        lane_p, row_p = iota((LANES, 85), 1), iota((LANES, 85), 0)
        pmask = (lane_p == 0) | ((lane_p + 3) % 4 == (row_p >> 5))
        pa[...] = jnp.zeros_like(pa)
        for ax in range(3):
            w = (px_ref[ax] - 0.5) * SCALE
            w = jnp.where(pmask, jnp.concatenate([w, w, w, w], axis=0), 0.0)
            h, m, l = thirds(w)
            pa[pl.ds(ax, 24, stride=8), :] = (
                nt(pick, h.astype(BF16)) + nt(pick, m.astype(BF16)) + nt(pick, l.astype(BF16))
            )

    once(sec_prox)

    def basis_parts(q):
        hi, lo = halves(basis_ref[:, pl.ds(q * 256, 256)])
        mask = bmask[...]
        return (
            jnp.concatenate([hi, hi, hi, hi], axis=0) * mask,
            jnp.concatenate([lo, lo, lo, lo], axis=0) * mask,
        )

    loads["basis"].wait()
    loads["rhs"].wait()
    coef3 = gc

    def leaf_coef(q, c):
        bh, bl = basis_parts(q)
        v = stacked(rhs_ref[:, pl.ds(q * 256, 256)])
        coef3[5 + q] = folded(nt(v, bh) + nt(v, bl))
        return c

    lax.fori_loop(0, 16, leaf_coef, 0, unroll=4)

    loads["tr"].wait()
    lane_n, row_n = iota((LANES, 84), 1), iota((LANES, 84), 0)
    tmask = (lane_n < 4) | (((lane_n >> 2) + 3) % 4 == (row_n >> 5))
    eye88 = jnp.where(iota((88, 84), 0) == iota((88, 84), 1), 1.0, 0.0).astype(BF16)

    bit = [(iota((8, LANES), 0) & k) == 0 for k in (1, 2, 4)]

    def turn(g, c):
        wide = []
        for i in range(8):
            w = tr_ref[8 * g + i]
            w = jnp.where(tmask, jnp.concatenate([w, w, w, w], axis=0), 0.0)
            hi, lo = halves(w)
            wide.append(nt(eye88, hi) + nt(eye88, lo))
        for n in range(0, 84, 8):
            v = [w[n : n + 8] for w in wide]
            for p, k in ((2, 4), (1, 2), (0, 1)):
                for i in range(8):
                    if not i & k:
                        x, y = v[i], v[i + k]
                        v[i] = jnp.where(bit[p], x, pltpu.roll(y, k, axis=0))
                        v[i + k] = jnp.where(bit[p], pltpu.roll(x, 8 - k, axis=0), y)
            for i in range(min(8, 84 - n)):
                tb[pl.ds(pl.multiple_of((n + i) * 32 + 8 * g, 8), 8), :] = v[i]
        return c

    lax.fori_loop(0, 4, turn, 0, unroll=2)

    def part(i, c):
        hi, lo = halves(tb[pl.ds(i * LANES, LANES), :])
        tbh[i] = hi
        tbl[i] = lo
        return c

    lax.fori_loop(0, 21, part, 0, unroll=3)

    def sec_up():
        for r in range(4):
            acc = jnp.zeros((32, LANES), F32)
            for i in range(4):
                b = stacked(coef3[5 + 4 * r + i])
                acc += nn(b, tbh[5 + 4 * r + i]) + nn(b, tbl[5 + 4 * r + i])
            coef3[1 + r] = folded(acc)
        acc = jnp.zeros((32, LANES), F32)
        for i in range(4):
            b = stacked(coef3[1 + i])
            acc += nn(b, tbh[1 + i]) + nn(b, tbl[1 + i])
        coef3[0] = folded(acc)
        b = stacked(coef3[0])
        sq[0:16, :] = folded(nn(b, tbh[0]) + nn(b, tbl[0]))

    once(sec_up)

    pl.semaphore_wait(barrier, 7 + quads - 1)

    def remote(src, dst_ref, i, d):
        return pltpu.make_async_remote_copy(
            src_ref=src, dst_ref=dst_ref, send_sem=sem_s.at[i], recv_sem=sem_r.at[i],
            device_id=(d,), device_id_type=MESH,
        )

    def sec_pack():
        sq[16:24, :] = source_rows(pa[21 * 8 : 22 * 8, :])
        for i, (to_left, to_right) in enumerate(((5, 19), (6, 20), (1, 3), (2, 4), (0, 0))):
            for side, u in ((0, to_left), (1, to_right)):
                sl[side, i, 0:16, :] = coef3[u]
                sl[side, i, 16:24, :] = source_rows(pa[u * 8 : u * 8 + 8, :])
        s1[0:16, :] = coef3[0]
        s1[16:24, :] = source_rows(pa[0:8, :])

    once(sec_pack)

    rq[seat] = sq[...]
    quad_copies = [
        pltpu.make_async_remote_copy(
            src_ref=sq, dst_ref=rq.at[seat], send_sem=sem_s.at[6 + o], recv_sem=sem_r.at[6 + seat],
            device_id=(peers[o],), device_id_type=MESH,
        )
        for o in range(3)
    ]
    for c in quad_copies:
        c.start()
    level_copies = [
        remote(sl.at[0], rlr.at[1], 2, left),
        remote(sl.at[1], rlr.at[0], 3, right),
        remote(s1, r1.at[1], 4, left2),
        remote(s1, r1.at[0], 5, right2),
    ]
    for c in level_copies:
        c.start()

    loads["pts"].wait()
    p8[...] = jnp.zeros_like(p8)
    p8[0:3, :] = (pts_ref[...] - 0.5) * SCALE
    for i, u in ((0, 0), (1, 31)):
        sn[i, 0:16, :] = rhs_ref[:, u * LANES : (u + 1) * LANES]
        sn[i, 16:24, :] = source_rows(p8[:, u * LANES : (u + 1) * LANES])

    near_copies = [
        remote(sn.at[0], rn.at[1], 0, left),
        remote(sn.at[1], rn.at[0], 1, right),
    ]
    for c in near_copies:
        c.start()

    for name in ("nl", "cl", "rl"):
        loads[name].wait()

    clb[...] = jnp.full_like(clb, -BIG)
    clb[0:20, 0:84] = jnp.where(cl_ref[...] >= 0, 0.0, -BIG)
    nlb[...] = jnp.full_like(nlb, -BIG)
    nlb[0:5, 0:64] = jnp.where(nl_ref[...] >= 0, 0.0, -BIG)
    nb = nlb[...]
    h = iota((8, LANES), 1) % 4
    for k in range(1, 4):
        nb = jnp.where(h == k, pltpu.roll(nlb[...], k, axis=0), nb)
    nlb[...] = nb
    cb = clb[...]
    clb[...] = jnp.where((iota((32, LANES), 1) + 4) % 8 >= 4, pltpu.roll(cb, 4, axis=0), cb)
    c1b = cb
    sel8 = jnp.where(iota((LANES, 256), 0) == iota((LANES, 256), 1) >> 5, 1.0, 0.0).astype(BF16)
    sel4 = jnp.where(iota((LANES, 256), 0) == iota((LANES, 256), 1) >> 6, 1.0, 0.0).astype(BF16)
    selm = jnp.where(iota((LANES, LANES), 0) % 4 == iota((LANES, LANES), 1) >> 5, 1.0, 0.0).astype(BF16)
    rlist = jnp.where(rl_ref[...] >= 0, 0.0, -BIG) + jnp.zeros((32, LANES), F32)
    rlist = jnp.where(iota((32, LANES), 1) >> 2 == iota((32, LANES), 0), rlist, 0.0)
    rb[...] = nn(rlist.astype(BF16), selm)

    def near_source(slab, values, rows):
        cls = (2 * slab + (iota((8, LANES), 1) >> 6)) % 8
        hot = jnp.where(iota((8, LANES), 0) == cls, 1.0, 0.0)
        f = jnp.concatenate([*source_stack(rows), hot, jnp.zeros((8, LANES), F32)], axis=0)
        ytn[pl.ds(pl.multiple_of(slab * LANES, LANES), LANES), :] = nt(eye_ref[...], f.astype(BF16)).astype(BF16)
        chn[slab] = stacked(values)

    def near_prep(v, c):
        for i in range(2):
            at = pl.ds(pl.multiple_of((2 * v + i) * LANES, LANES), LANES)
            near_source(2 * v + i + 1, rhs_ref[:, at], source_rows(p8[:, at]))
        x = p8[:, pl.ds(pl.multiple_of(v * 256, 256), 256)]
        bias = pltpu.roll(pltpu.roll(nlb[...], (LANES - 4 * v) % LANES, axis=1), (4 * v) % 8, axis=0)
        bias = nn(bias.astype(BF16), sel4)
        xn[v] = jnp.concatenate(
            [*target_stack(target_rows(x)), bias, jnp.zeros((8, 256), F32)], axis=0).astype(BF16)
        return c

    lax.fori_loop(0, 16, near_prep, 0, unroll=4)

    def near_unit(v, c):
        gh, gl = gauss(nn(ytn[pl.ds(pl.multiple_of(v * 256, 256), 512), :], xn[v]))
        b = jnp.concatenate([chn[2 * v + i] for i in range(4)], axis=1)
        nr[:, pl.ds(pl.multiple_of(v * 256, 256), 256)] = folded(nn(b, gh) + nn(b, gl))
        return c

    lax.fori_loop(1, 7, near_unit, 0, unroll=3)

    for o in range(3):
        quad_copies[o].wait_send()
    for o in range(1, 4):
        frm = (seat + o) % 4
        pltpu.make_async_remote_copy(
            src_ref=sq, dst_ref=rq.at[frm], send_sem=sem_s.at[6], recv_sem=sem_r.at[6 + frm],
            device_id=(left,), device_id_type=MESH,
        ).wait_recv()
    group = iota((24, LANES), 1) >> 5
    merged = jnp.where(group == 0, rq[0], jnp.where(group == 1, rq[1], jnp.where(group == 2, rq[2], rq[3])))
    sq2[...] = merged
    rg[quad] = merged

    def root_copy(o, slot):
        return pltpu.make_async_remote_copy(
            src_ref=sq2, dst_ref=rg.at[slot], send_sem=gs_sem.at[o], recv_sem=gr_sem.at[slot],
            device_id=(dst(o),), device_id_type=MESH,
        )

    def root_send(o, c):
        root_copy(o, quad).start()
        return c

    lax.fori_loop(1, quads, root_send, 0)

    lax.fori_loop(7, 15, near_unit, 0, unroll=4)

    def level_source(slab, q_class, values, rows):
        cls = (4 * q_class + (iota((32, LANES), 1) >> 5)) % 32
        hot = jnp.where(iota((32, LANES), 0) == cls, 1.0, 0.0)
        f = jnp.concatenate([*source_stack(rows), hot], axis=0)
        at = slab * LANES if isinstance(slab, int) else pl.multiple_of(slab * LANES, LANES)
        ytc[pl.ds(at, LANES), :] = nt(eye_ref[...], f.astype(BF16)).astype(BF16)
        chc[slab] = stacked(values)

    def level_prep(w, c):
        q = jnp.where(w < 8, 2 * w, 2 * w - 16)
        u = q + jnp.where(w < 8, 5, 1)
        slab = q + jnp.where(w < 8, 2, 22)
        xs = [pa[pl.ds(pl.multiple_of((u + i) * 8, 8), 8), :] for i in range(2)]
        for i in range(2):
            level_source(slab + i, q + 2 + i, coef3[u + i], source_rows(xs[i]))
        bias = pltpu.roll(pltpu.roll(clb[...], (LANES - 4 * u) % LANES, axis=1), (4 * q) % 32, axis=0)
        bias = nn(bias.astype(BF16), sel8)
        xs = target_rows(jnp.concatenate(xs, axis=1))
        xc[w] = jnp.concatenate([*target_stack(xs), bias], axis=0).astype(BF16)
        return c

    lax.fori_loop(0, 10, level_prep, 0, unroll=2)
    level_source(30, 2, coef3[0], source_rows(pa[0:8, :]))
    bias = nn(c1b.astype(BF16), sel8[:, 0:LANES])
    xc1[...] = jnp.concatenate([*target_stack(target_rows(pa[0:8, :])), bias], axis=0).astype(BF16)
    for c in level_copies:
        c.wait()
    def sec_halo():
        for i in range(2):
            for first, k, n in ((0, 0, 16), (20, 2, 4)):
                level_source(first + i, i, rlr[0, k + i, 0:16, :], rlr[0, k + i, 16:24, :])
                level_source(first + 2 + n + i, 2 + n + i, rlr[1, k + i, 0:16, :], rlr[1, k + i, 16:24, :])
        for i, blk in ((0, r1[0]), (1, rlr[0, 4]), (3, rlr[1, 4]), (4, r1[1])):
            level_source(28 + i, i, blk[0:16], blk[16:24])

    once(sec_halo)

    def couple_unit(w, c):
        q = jnp.where(w < 8, 2 * w, 2 * w - 16)
        u = q + jnp.where(w < 8, 5, 1)
        slab = q + jnp.where(w < 8, 0, 20)
        gh, gl = gauss(nn(ytc[pl.ds(pl.multiple_of(slab * LANES, LANES), 6 * LANES), :], xc[w]))
        b = jnp.concatenate([chc[slab + i] for i in range(6)], axis=1)
        g = folded(nn(b, gh) + nn(b, gl))
        fc[u] = g[:, 0:LANES]
        fc[u + 1] = g[:, LANES:256]
        return c

    lax.fori_loop(0, 10, couple_unit, 0, unroll=5)
    def sec_l1():
        gh, gl = gauss(nn(ytc[28 * LANES : 33 * LANES, :], xc1[...]))
        b = jnp.concatenate([chc[28 + i] for i in range(5)], axis=1)
        fc[0] = folded(nn(b, gh) + nn(b, gl))

    once(sec_l1)

    for c in near_copies:
        c.wait()
    near_source(0, rn[0, 0:16, :], rn[0, 16:24, :])
    near_source(33, rn[1, 0:16, :], rn[1, 16:24, :])

    near_unit(0, 0)
    near_unit(15, 0)

    froot = jnp.concatenate(target_stack(target_rows(pa[21 * 8 : 22 * 8, :])), axis=0)
    troot = nt(eye_ref[0:32, :], froot.astype(BF16)).astype(BF16)

    def root_wait(o, c):
        root_copy(o, (quad + quads - o) % quads).wait_recv()
        return c

    lax.fori_loop(1, quads, root_wait, 0)

    def sec_tail():
        batch = min(8, quads)

        def root_unit(i, acc):
            us = [i * batch + j for j in range(batch)]
            rows = jnp.concatenate([rg[u, 16:24, :] for u in us], axis=1)
            f = jnp.concatenate(source_stack(rows), axis=0).astype(BF16)
            bias = jnp.concatenate([rb[pl.ds(u, 1), :] for u in us], axis=1)
            gh, gl = gauss(nn(troot, f) + bias)
            v = stacked(jnp.concatenate([rg[u, 0:16, :] for u in us], axis=1))
            return acc + nt(v, jnp.concatenate([gh, gl], axis=0))

        acc = jnp.zeros((32, 64), F32)
        for i in range(quads // batch):
            acc = root_unit(i, acc)
        acc = folded(acc)
        f0 = jnp.concatenate([acc, jnp.zeros((16, 64), F32)], axis=1)

        def down(f, u):
            b = stacked(f)
            return fc[u] + folded(nt(b, tbh[u]) + nt(b, tbl[u]))

        f1 = stacked(down(f0, 0))
        w = [t[1:5].reshape(512, LANES) for t in (tbh, tbl)]
        f2 = folded(nt(f1, w[0]) + nt(f1, w[1]))
        for r in range(4):
            b = stacked(fc[1 + r] + f2[:, r * LANES : (r + 1) * LANES])
            w = [t[5 + 4 * r : 9 + 4 * r].reshape(512, LANES) for t in (tbh, tbl)]
            f3 = folded(nt(b, w[0]) + nt(b, w[1]))
            for i in range(4):
                fd[4 * r + i] = stacked(fc[5 + 4 * r + i] + f3[:, i * LANES : (i + 1) * LANES])

    once(sec_tail)

    def far(q, c):
        at = pl.ds(pl.multiple_of(q * 256, 256), 256)
        bh, bl = basis_parts(q)
        b = fd[q]
        out_ref[:, at] = nr[:, at] + folded(nn(b, bh) + nn(b, bl))
        return c

    lax.fori_loop(0, 16, far, 0, unroll=8)

    def root_done(o, c):
        root_copy(o, quad).wait_send()
        return c

    lax.fori_loop(1, quads, root_done, 0)


def body(n_dev, points, rhs, leaf_basis, transfer, proxies, near_list, couple_list, root_list):
    rlist = root_list
    if n_dev < LANES:
        rlist = jnp.pad(rlist, ((0, 0), (0, LANES - n_dev)))
    quads = n_dev // 4
    ins = [(3, 4096), (16, 4096), (32, 4096), (32, 32, 84), (3, 32, 85), (5, 64), (20, 84), (1, LANES)]
    scratch = [
        *[pltpu.VMEM(shape, F32 if i < 5 else jnp.int32) for i, shape in enumerate(ins)],
        pltpu.SemaphoreType.DMA((8,)),
        pltpu.VMEM((16, 4096), F32),
        pltpu.VMEM((8, 4096), F32),
        pltpu.VMEM((192, LANES), F32),
        pltpu.VMEM((84 * 32, LANES), F32),
        pltpu.VMEM((21, LANES, LANES), BF16),
        pltpu.VMEM((21, LANES, LANES), BF16),
        pltpu.VMEM((LANES, LANES), BF16),
        pltpu.VMEM((LANES, 256), BF16),
        pltpu.VMEM((34 * LANES, KN), BF16),
        pltpu.VMEM((34, 32, LANES), BF16),
        pltpu.VMEM((16, KN, 256), BF16),
        pltpu.VMEM((33 * LANES, KC), BF16),
        pltpu.VMEM((33, 32, LANES), BF16),
        pltpu.VMEM((10, KC, 256), BF16),
        pltpu.VMEM((KC, LANES), BF16),
        pltpu.VMEM((32, LANES), F32),
        pltpu.VMEM((8, LANES), F32),
        pltpu.VMEM((32, LANES), F32),
        pltpu.VMEM((21, 16, LANES), F32),
        pltpu.VMEM((21, 16, LANES), F32),
        pltpu.VMEM((16, 32, LANES), BF16),
        pltpu.VMEM((2, 24, LANES), F32),
        pltpu.VMEM((2, 24, LANES), F32),
        pltpu.VMEM((2, 5, 24, LANES), F32),
        pltpu.VMEM((2, 5, 24, LANES), F32),
        pltpu.VMEM((24, LANES), F32),
        pltpu.VMEM((2, 24, LANES), F32),
        pltpu.VMEM((24, LANES), F32),
        pltpu.VMEM((24, LANES), F32),
        pltpu.VMEM((4, 24, LANES), F32),
        pltpu.VMEM((quads, 24, LANES), F32),
        pltpu.SemaphoreType.DMA((10,)),
        pltpu.SemaphoreType.DMA((10,)),
        pltpu.SemaphoreType.DMA((quads,)),
        pltpu.SemaphoreType.DMA((quads,)),
    ]
    vmem = pl.BlockSpec(memory_space=pltpu.VMEM)
    return pl.pallas_call(
        functools.partial(kernel, n_dev),
        out_shape=jax.ShapeDtypeStruct(rhs.shape, F32),
        in_specs=[pl.BlockSpec(memory_space=pltpu.HBM)] * 8,
        out_specs=vmem,
        scratch_shapes=scratch,
        compiler_params=pltpu.CompilerParams(
            collective_id=0, has_side_effects=True, vmem_limit_bytes=60 * 2**20
        ),
        name="hmatvec",
    )(points, rhs, leaf_basis, transfer, proxies, near_list.T, couple_list.T, rlist)


def solution(mesh):
    n_dev = mesh.shape["leaf"]
    in_specs = (
        P(None, "leaf"), P(None, "leaf"), P(None, "leaf"), P(None, None, "leaf"), P(None, None, "leaf"),
        P("leaf", None), P("leaf", None), P("leaf", None),
    )
    return jax.shard_map(
        functools.partial(body, n_dev), mesh=mesh, in_specs=in_specs, out_specs=P(None, "leaf"), check_vma=False
    )
```

```python
import functools
import math

import jax
import jax.numpy as jnp
from jax import lax
from jax.experimental import pallas as pl
from jax.experimental.pallas import tpu as pltpu
from jax.sharding import PartitionSpec as P

F32, BF16 = jnp.float32, jnp.bfloat16
MESH = pl.DeviceIdType.MESH
BIG = 16384.0
SCALE = math.sqrt(10.0 * math.log2(math.e))
LANES = 128
KN = 64
KC = 80


def nt(a, b):
    return lax.dot_general(a, b, (((1,), (1,)), ((), ())), preferred_element_type=F32)


def nn(a, b):
    return lax.dot_general(a, b, (((1,), (0,)), ((), ())), preferred_element_type=F32)


def iota(shape, dim):
    return lax.broadcasted_iota(jnp.int32, shape, dim)


def halves(x):
    hi = x.astype(BF16)
    return hi, (x - hi.astype(F32)).astype(BF16)


def stacked(x):
    hi = x.astype(BF16).astype(F32)
    return jnp.concatenate([hi, x - hi], axis=0).astype(BF16)


def folded(x):
    n = x.shape[0] // 2
    return x[:n] + x[n:]


def thirds(x):
    h = x.astype(BF16).astype(F32)
    m = (x - h).astype(BF16).astype(F32)
    return h, m, x - h - m


def source_rows(x):
    r = iota(x.shape, 0)
    x = jnp.where(r < 3, x, 0.0)
    n2 = jnp.sum(x * x, axis=0, keepdims=True)
    return jnp.where(r < 3, x, jnp.where(r == 3, n2, jnp.where(r == 4, 1.0, 0.0)))


def target_rows(x):
    r = iota(x.shape, 0)
    x = jnp.where(r < 3, x, 0.0)
    n2 = jnp.sum(x * x, axis=0, keepdims=True)
    return jnp.where(r < 3, 2.0 * x, jnp.where(r == 3, -1.0, jnp.where(r == 4, -n2, 0.0)))


def source_stack(rows):
    h, m, l = thirds(rows)
    return [h, m, l, h, m, h]


def target_stack(rows):
    h, m, l = thirds(rows)
    return [h, h, h, m, m, l]


def once(fn):
    fn()


def gauss(e):
    g = jnp.exp2(e)
    return halves(g)


def kernel(
    n_dev,
    pts_hbm, rhs_hbm, basis_hbm, tr_hbm, px_hbm, nl_hbm, cl_hbm, rl_hbm,
    out_ref,
    pts_ref, rhs_ref, basis_ref, tr_ref, px_ref, nl_ref, cl_ref, rl_ref, in_sem,
    nr, p8, pa, tb, tbh, tbl, eye_ref, bmask,
    ytn, chn, xn, ytc, chc, xc, xc1, clb, nlb, rb,
    gc, fc, fd,
    sn, rn, sl, rlr, s1, r1, sq, sq2, rq, rg,
    sem_s, sem_r, gs_sem, gr_sem,
):
    loads = {
        name: pltpu.make_async_copy(src, dst, in_sem.at[i])
        for i, (name, src, dst) in enumerate((
            ("px", px_hbm, px_ref), ("basis", basis_hbm, basis_ref), ("rhs", rhs_hbm, rhs_ref),
            ("tr", tr_hbm, tr_ref), ("pts", pts_hbm, pts_ref), ("nl", nl_hbm, nl_ref),
            ("cl", cl_hbm, cl_ref), ("rl", rl_hbm, rl_ref),
        ))
    }
    for c in loads.values():
        c.start()
    me = lax.axis_index("leaf")
    groups = n_dev // 8
    group, seat = me // 8, me % 8
    left, right = (me + n_dev - 1) % n_dev, (me + 1) % n_dev
    left2, right2 = (me + n_dev - 2) % n_dev, (me + 2) % n_dev
    peers = [group * 8 + (seat + o) % 8 for o in range(1, 8)]

    def dst(o):
        return ((group + o) % groups) * 8 + seat

    barrier = pltpu.get_barrier_semaphore()
    for d in [left, right, left2, right2, *peers]:
        pl.semaphore_signal(barrier, inc=1, device_id=(d,), device_id_type=MESH)

    def greet(o, c):
        pl.semaphore_signal(barrier, inc=1, device_id=(dst(o),), device_id_type=MESH)
        return c

    lax.fori_loop(1, groups, greet, 0)

    def sec_const():
        eye_ref[...] = jnp.where(iota((LANES, LANES), 0) == iota((LANES, LANES), 1), 1.0, 0.0).astype(BF16)
        bmask[...] = jnp.where(iota((LANES, 256), 0) // 32 == iota((LANES, 256), 1) // 64, 1.0, 0.0).astype(BF16)

    once(sec_const)

    loads["px"].wait()
    def sec_prox():
        pick = jnp.where(
            ((iota((24, 85), 1) >= 1) & ((iota((24, 85), 1) - 1) >> 2 == iota((24, 85), 0)))
            | ((iota((24, 85), 1) == 0) & (iota((24, 85), 0) == 21)), 1.0, 0.0).astype(BF16)
        lane_p, row_p = iota((LANES, 85), 1), iota((LANES, 85), 0)
        pmask = (lane_p == 0) | ((lane_p + 3) % 4 == (row_p >> 5))
        pa[...] = jnp.zeros_like(pa)
        for ax in range(3):
            w = (px_ref[ax] - 0.5) * SCALE
            w = jnp.where(pmask, jnp.concatenate([w, w, w, w], axis=0), 0.0)
            h, m, l = thirds(w)
            pa[pl.ds(ax, 24, stride=8), :] = (
                nt(pick, h.astype(BF16)) + nt(pick, m.astype(BF16)) + nt(pick, l.astype(BF16))
            )

    once(sec_prox)

    def basis_parts(q):
        hi, lo = halves(basis_ref[:, pl.ds(q * 256, 256)])
        mask = bmask[...]
        return (
            jnp.concatenate([hi, hi, hi, hi], axis=0) * mask,
            jnp.concatenate([lo, lo, lo, lo], axis=0) * mask,
        )

    loads["basis"].wait()
    loads["rhs"].wait()
    coef3 = gc

    def leaf_coef(q, c):
        bh, bl = basis_parts(q)
        v = stacked(rhs_ref[:, pl.ds(q * 256, 256)])
        coef3[5 + q] = folded(nt(v, bh) + nt(v, bl))
        return c


    loads["tr"].wait()
    lane_n, row_n = iota((LANES, 84), 1), iota((LANES, 84), 0)
    tmask = (lane_n < 4) | (((lane_n >> 2) + 3) % 4 == (row_n >> 5))
    tmask = jnp.where(tmask, 1.0, 0.0).astype(BF16)
    eye88 = jnp.where(iota((88, 84), 0) == iota((88, 84), 1), 1.0, 0.0).astype(BF16)

    bit = [(iota((8, LANES), 0) & k) == 0 for k in (1, 2, 4)]

    def turn(g, c):
        wide = []
        for i in range(8):
            w = tr_ref[8 * g + i]
            hi, lo = [jnp.concatenate([x, x, x, x], axis=0) * tmask for x in halves(w)]
            wide.append(nt(eye88, hi) + nt(eye88, lo))
        for n in range(0, 84, 8):
            v = [w[n : n + 8] for w in wide]
            for p, k in ((2, 4), (1, 2), (0, 1)):
                for i in range(8):
                    if not i & k:
                        x, y = v[i], v[i + k]
                        v[i] = jnp.where(bit[p], x, pltpu.roll(y, k, axis=0))
                        v[i + k] = jnp.where(bit[p], pltpu.roll(x, 8 - k, axis=0), y)
            for i in range(min(8, 84 - n)):
                tb[pl.ds(pl.multiple_of((n + i) * 32 + 8 * g, 8), 8), :] = v[i]
        for i in range(4):
            leaf_coef(4 * g + i, 0)
        return c

    lax.fori_loop(0, 4, turn, 0, unroll=2)

    def part(i, c):
        hi, lo = halves(tb[pl.ds(i * LANES, LANES), :])
        tbh[i] = hi
        tbl[i] = lo
        return c

    lax.fori_loop(0, 21, part, 0, unroll=3)

    def sec_up():
        for r in range(4):
            acc = jnp.zeros((32, LANES), F32)
            for i in range(4):
                b = stacked(coef3[5 + 4 * r + i])
                acc += nn(b, tbh[5 + 4 * r + i]) + nn(b, tbl[5 + 4 * r + i])
            coef3[1 + r] = folded(acc)
        acc = jnp.zeros((32, LANES), F32)
        for i in range(4):
            b = stacked(coef3[1 + i])
            acc += nn(b, tbh[1 + i]) + nn(b, tbl[1 + i])
        coef3[0] = folded(acc)
        b = stacked(coef3[0])
        sq[0:16, :] = folded(nn(b, tbh[0]) + nn(b, tbl[0]))

    once(sec_up)

    pl.semaphore_wait(barrier, 11 + groups - 1)

    def remote(src, dst_ref, i, d):
        return pltpu.make_async_remote_copy(
            src_ref=src, dst_ref=dst_ref, send_sem=sem_s.at[i], recv_sem=sem_r.at[i],
            device_id=(d,), device_id_type=MESH,
        )

    def sec_pack():
        sq[16:19, :] = pa[21 * 8 : 21 * 8 + 3, :]
        for i, (to_left, to_right) in enumerate(((5, 19), (6, 20), (1, 3), (2, 4), (0, 0))):
            for side, u in ((0, to_left), (1, to_right)):
                sl[side, i, 0:16, :] = coef3[u]
                sl[side, i, 16:24, :] = source_rows(pa[u * 8 : u * 8 + 8, :])
        s1[0:16, :] = coef3[0]
        s1[16:24, :] = source_rows(pa[0:8, :])

    once(sec_pack)

    rq[seat] = sq[...]
    group_copies = [
        pltpu.make_async_remote_copy(
            src_ref=sq, dst_ref=rq.at[seat], send_sem=sem_s.at[6 + o], recv_sem=sem_r.at[6 + seat],
            device_id=(peers[o],), device_id_type=MESH,
        )
        for o in range(7)
    ]
    for c in group_copies:
        c.start()
    level_copies = [
        remote(sl.at[0], rlr.at[1], 2, left),
        remote(sl.at[1], rlr.at[0], 3, right),
        remote(s1, r1.at[1], 4, left2),
        remote(s1, r1.at[0], 5, right2),
    ]
    for c in level_copies:
        c.start()

    loads["pts"].wait()
    p8[...] = jnp.zeros_like(p8)
    p8[0:3, :] = (pts_ref[...] - 0.5) * SCALE
    for i, u in ((0, 0), (1, 31)):
        sn[i, 0:16, :] = rhs_ref[:, u * LANES : (u + 1) * LANES]
        sn[i, 16:24, :] = source_rows(p8[:, u * LANES : (u + 1) * LANES])

    near_copies = [
        remote(sn.at[0], rn.at[1], 0, left),
        remote(sn.at[1], rn.at[0], 1, right),
    ]
    for c in near_copies:
        c.start()

    for name in ("nl", "cl", "rl"):
        loads[name].wait()

    clb[...] = jnp.full_like(clb, -BIG)
    clb[0:20, 0:84] = jnp.where(cl_ref[...] >= 0, 0.0, -BIG)
    nlb[...] = jnp.full_like(nlb, -BIG)
    nlb[0:5, 0:64] = jnp.where(nl_ref[...] >= 0, 0.0, -BIG)
    nb = nlb[...]
    h = iota((8, LANES), 1) % 4
    for k in range(1, 4):
        nb = jnp.where(h == k, pltpu.roll(nlb[...], k, axis=0), nb)
    nlb[...] = nb
    cb = clb[...]
    clb[...] = jnp.where((iota((32, LANES), 1) + 4) % 8 >= 4, pltpu.roll(cb, 4, axis=0), cb)
    c1b = cb
    sel8 = jnp.where(iota((LANES, 256), 0) == iota((LANES, 256), 1) >> 5, 1.0, 0.0).astype(BF16)
    sel4 = jnp.where(iota((LANES, 256), 0) == iota((LANES, 256), 1) >> 6, 1.0, 0.0).astype(BF16)
    selm = jnp.where(iota((LANES, LANES), 0) % 4 == iota((LANES, LANES), 1) >> 5, 1.0, 0.0).astype(BF16)
    rlist = jnp.where(rl_ref[...] >= 0, 0.0, -BIG) + jnp.zeros((32, LANES), F32)
    rlist = jnp.where(iota((32, LANES), 1) >> 2 == iota((32, LANES), 0), rlist, 0.0)
    rb[...] = nn(rlist.astype(BF16), selm)

    def near_source(slab, values, rows):
        cls = (2 * slab + (iota((8, LANES), 1) >> 6)) % 8
        hot = jnp.where(iota((8, LANES), 0) == cls, 1.0, 0.0)
        f = jnp.concatenate([*source_stack(rows), hot, jnp.zeros((8, LANES), F32)], axis=0)
        ytn[pl.ds(pl.multiple_of(slab * LANES, LANES), LANES), :] = nt(eye_ref[...], f.astype(BF16)).astype(BF16)
        chn[slab] = stacked(values)

    def near_prep(v, c):
        for i in range(2):
            at = pl.ds(pl.multiple_of((2 * v + i) * LANES, LANES), LANES)
            near_source(2 * v + i + 1, rhs_ref[:, at], source_rows(p8[:, at]))
        x = p8[:, pl.ds(pl.multiple_of(v * 256, 256), 256)]
        bias = pltpu.roll(pltpu.roll(nlb[...], (LANES - 4 * v) % LANES, axis=1), (4 * v) % 8, axis=0)
        bias = nn(bias.astype(BF16), sel4)
        xn[v] = jnp.concatenate(
            [*target_stack(target_rows(x)), bias, jnp.zeros((8, 256), F32)], axis=0).astype(BF16)
        return c

    lax.fori_loop(0, 16, near_prep, 0, unroll=4)

    def chunked(feats, first, targets, values, slab, chunks):
        acc = None
        for i in range(chunks):
            at = pl.ds(pl.multiple_of(first + i * 256, 256), 256)
            gh, gl = gauss(nn(feats[at, :], targets))
            b = jnp.concatenate([values[slab + 2 * i], values[slab + 2 * i + 1]], axis=1)
            y = nn(b, gh) + nn(b, gl)
            acc = y if acc is None else acc + y
        return folded(acc)

    def near_unit(v, c):
        y = chunked(ytn, v * 256, xn[v], chn, 2 * v, 2)
        nr[:, pl.ds(pl.multiple_of(v * 256, 256), 256)] = y
        return c

    lax.fori_loop(1, 7, near_unit, 0, unroll=3)

    for o in range(7):
        group_copies[o].wait_send()
    for o in range(1, 8):
        frm = (seat + o) % 8
        pltpu.make_async_remote_copy(
            src_ref=sq, dst_ref=rq.at[frm], send_sem=sem_s.at[6], recv_sem=sem_r.at[6 + frm],
            device_id=(left,), device_id_type=MESH,
        ).wait_recv()
    place = iota((19, LANES), 1) >> 5
    for i in range(2):
        blocks = [rq[4 * i + j] for j in range(4)]
        merged = blocks[3]
        for j in range(3):
            merged = jnp.where(place == j, blocks[j], merged)
        sq2[i] = merged
        rg[group, i] = merged

    def root_send(o, c):
        pltpu.make_async_remote_copy(
            src_ref=sq2, dst_ref=rg.at[group], send_sem=gs_sem.at[0], recv_sem=gr_sem.at[0],
            device_id=(dst(o),), device_id_type=MESH,
        ).start()
        return c

    lax.fori_loop(1, groups, root_send, 0)

    lax.fori_loop(7, 15, near_unit, 0, unroll=4)

    def level_source(slab, q_class, values, rows):
        cls = (4 * q_class + (iota((32, LANES), 1) >> 5)) % 32
        hot = jnp.where(iota((32, LANES), 0) == cls, 1.0, 0.0)
        f = jnp.concatenate([*source_stack(rows), hot], axis=0)
        at = slab * LANES if isinstance(slab, int) else pl.multiple_of(slab * LANES, LANES)
        ytc[pl.ds(at, LANES), :] = nt(eye_ref[...], f.astype(BF16)).astype(BF16)
        chc[slab] = stacked(values)

    def level_prep(w, c):
        q = jnp.where(w < 8, 2 * w, 2 * w - 16)
        u = q + jnp.where(w < 8, 5, 1)
        slab = q + jnp.where(w < 8, 2, 22)
        xs = [pa[pl.ds(pl.multiple_of((u + i) * 8, 8), 8), :] for i in range(2)]
        for i in range(2):
            level_source(slab + i, q + 2 + i, coef3[u + i], source_rows(xs[i]))
        bias = pltpu.roll(pltpu.roll(clb[...], (LANES - 4 * u) % LANES, axis=1), (4 * q) % 32, axis=0)
        bias = nn(bias.astype(BF16), sel8)
        xs = target_rows(jnp.concatenate(xs, axis=1))
        xc[w] = jnp.concatenate([*target_stack(xs), bias], axis=0).astype(BF16)
        return c

    lax.fori_loop(0, 10, level_prep, 0, unroll=5)
    level_source(30, 2, coef3[0], source_rows(pa[0:8, :]))
    bias = nn(c1b.astype(BF16), sel8[:, 0:LANES])
    xc1[...] = jnp.concatenate([*target_stack(target_rows(pa[0:8, :])), bias], axis=0).astype(BF16)
    for c in level_copies:
        c.wait()
    def sec_halo():
        for i in range(2):
            for first, k, n in ((0, 0, 16), (20, 2, 4)):
                level_source(first + i, i, rlr[0, k + i, 0:16, :], rlr[0, k + i, 16:24, :])
                level_source(first + 2 + n + i, 2 + n + i, rlr[1, k + i, 0:16, :], rlr[1, k + i, 16:24, :])
        for i, blk in ((0, r1[0]), (1, rlr[0, 4]), (3, rlr[1, 4]), (4, r1[1])):
            level_source(28 + i, i, blk[0:16], blk[16:24])

    once(sec_halo)

    def couple_unit(w, c):
        q = jnp.where(w < 8, 2 * w, 2 * w - 16)
        u = q + jnp.where(w < 8, 5, 1)
        slab = q + jnp.where(w < 8, 0, 20)
        g = chunked(ytc, slab * LANES, xc[w], chc, slab, 3)
        fc[u] = g[:, 0:LANES]
        fc[u + 1] = g[:, LANES:256]
        return c

    lax.fori_loop(0, 10, couple_unit, 0, unroll=5)
    def sec_l1():
        gh, gl = gauss(nn(ytc[28 * LANES : 33 * LANES, :], xc1[...]))
        b = jnp.concatenate([chc[28 + i] for i in range(5)], axis=1)
        fc[0] = folded(nn(b, gh) + nn(b, gl))

    once(sec_l1)

    for c in near_copies:
        c.wait()
    near_source(0, rn[0, 0:16, :], rn[0, 16:24, :])
    near_source(33, rn[1, 0:16, :], rn[1, 16:24, :])

    near_unit(0, 0)
    near_unit(15, 0)

    froot = jnp.concatenate(target_stack(target_rows(pa[21 * 8 : 22 * 8, :])), axis=0)
    troot = nt(eye_ref[0:32, :], froot.astype(BF16)).astype(BF16)

    if groups > 1:
        others = rg.at[pl.ds(0, groups - 1)]
        pltpu.make_async_copy(others, others, gr_sem.at[0]).wait()

    def sec_tail():
        batch = min(8, 2 * groups)

        def root_unit(i, acc):
            us = [(i * batch + j) // 2 for j in range(batch)]
            rows = jnp.concatenate([rg[u, j % 2, 16:19, :] for j, u in enumerate(us)], axis=1)
            rows = source_rows(jnp.concatenate([rows, jnp.zeros((5, rows.shape[1]), F32)], axis=0))
            f = jnp.concatenate(source_stack(rows), axis=0).astype(BF16)
            bias = jnp.concatenate([rb[pl.ds(i * batch + j, 1), :] for j in range(batch)], axis=1)
            gh, gl = gauss(nn(troot, f) + bias)
            v = stacked(jnp.concatenate([rg[u, j % 2, 0:16, :] for j, u in enumerate(us)], axis=1))
            return acc + nt(v, jnp.concatenate([gh, gl], axis=0))

        acc = jnp.zeros((32, 64), F32)
        for i in range(2 * groups // batch):
            acc = root_unit(i, acc)
        acc = folded(acc)
        f0 = jnp.concatenate([acc, jnp.zeros((16, 64), F32)], axis=1)

        def down(f, u):
            b = stacked(f)
            return fc[u] + folded(nt(b, tbh[u]) + nt(b, tbl[u]))

        f1 = stacked(down(f0, 0))
        w = [t[1:5].reshape(512, LANES) for t in (tbh, tbl)]
        f2 = folded(nt(f1, w[0]) + nt(f1, w[1]))
        for r in range(4):
            b = stacked(fc[1 + r] + f2[:, r * LANES : (r + 1) * LANES])
            w = [t[5 + 4 * r : 9 + 4 * r].reshape(512, LANES) for t in (tbh, tbl)]
            f3 = folded(nt(b, w[0]) + nt(b, w[1]))
            for i in range(4):
                fd[4 * r + i] = stacked(fc[5 + 4 * r + i] + f3[:, i * LANES : (i + 1) * LANES])

    once(sec_tail)

    def far(q, c):
        at = pl.ds(pl.multiple_of(q * 256, 256), 256)
        bh, bl = basis_parts(q)
        b = fd[q]
        out_ref[:, at] = nr[:, at] + folded(nn(b, bh) + nn(b, bl))
        return c

    lax.fori_loop(0, 16, far, 0, unroll=8)

    if groups > 1:
        others = rg.at[pl.ds(0, groups - 1)]
        pltpu.make_async_copy(others, others, gs_sem.at[0]).wait()


def body(n_dev, points, rhs, leaf_basis, transfer, proxies, near_list, couple_list, root_list):
    rlist = root_list
    if n_dev < LANES:
        rlist = jnp.pad(rlist, ((0, 0), (0, LANES - n_dev)))
    groups = n_dev // 8
    ins = [(3, 4096), (16, 4096), (32, 4096), (32, 32, 84), (3, 32, 85), (5, 64), (20, 84), (1, LANES)]
    scratch = [
        *[pltpu.VMEM(shape, F32 if i < 5 else jnp.int32) for i, shape in enumerate(ins)],
        pltpu.SemaphoreType.DMA((8,)),
        pltpu.VMEM((16, 4096), F32),
        pltpu.VMEM((8, 4096), F32),
        pltpu.VMEM((192, LANES), F32),
        pltpu.VMEM((84 * 32, LANES), F32),
        pltpu.VMEM((21, LANES, LANES), BF16),
        pltpu.VMEM((21, LANES, LANES), BF16),
        pltpu.VMEM((LANES, LANES), BF16),
        pltpu.VMEM((LANES, 256), BF16),
        pltpu.VMEM((34 * LANES, KN), BF16),
        pltpu.VMEM((34, 32, LANES), BF16),
        pltpu.VMEM((16, KN, 256), BF16),
        pltpu.VMEM((33 * LANES, KC), BF16),
        pltpu.VMEM((33, 32, LANES), BF16),
        pltpu.VMEM((10, KC, 256), BF16),
        pltpu.VMEM((KC, LANES), BF16),
        pltpu.VMEM((32, LANES), F32),
        pltpu.VMEM((8, LANES), F32),
        pltpu.VMEM((32, LANES), F32),
        pltpu.VMEM((21, 16, LANES), F32),
        pltpu.VMEM((21, 16, LANES), F32),
        pltpu.VMEM((16, 32, LANES), BF16),
        pltpu.VMEM((2, 24, LANES), F32),
        pltpu.VMEM((2, 24, LANES), F32),
        pltpu.VMEM((2, 5, 24, LANES), F32),
        pltpu.VMEM((2, 5, 24, LANES), F32),
        pltpu.VMEM((24, LANES), F32),
        pltpu.VMEM((2, 24, LANES), F32),
        pltpu.VMEM((19, LANES), F32),
        pltpu.VMEM((2, 19, LANES), F32),
        pltpu.VMEM((8, 19, LANES), F32),
        pltpu.VMEM((groups, 2, 19, LANES), F32),
        pltpu.SemaphoreType.DMA((14,)),
        pltpu.SemaphoreType.DMA((14,)),
        pltpu.SemaphoreType.DMA((1,)),
        pltpu.SemaphoreType.DMA((1,)),
    ]
    vmem = pl.BlockSpec(memory_space=pltpu.VMEM)
    return pl.pallas_call(
        functools.partial(kernel, n_dev),
        out_shape=jax.ShapeDtypeStruct(rhs.shape, F32),
        in_specs=[pl.BlockSpec(memory_space=pltpu.HBM)] * 8,
        out_specs=vmem,
        scratch_shapes=scratch,
        compiler_params=pltpu.CompilerParams(
            collective_id=0, has_side_effects=True, vmem_limit_bytes=60 * 2**20
        ),
        name="hmatvec",
    )(points, rhs, leaf_basis, transfer, proxies, near_list.T, couple_list.T, rlist)


def solution(mesh):
    n_dev = mesh.shape["leaf"]
    in_specs = (
        P(None, "leaf"), P(None, "leaf"), P(None, "leaf"), P(None, None, "leaf"), P(None, None, "leaf"),
        P("leaf", None), P("leaf", None), P("leaf", None),
    )
    return jax.shard_map(
        functools.partial(body, n_dev), mesh=mesh, in_specs=in_specs, out_specs=P(None, "leaf"), check_vma=False
    )
```

```python
import functools
import math

import jax
import jax.numpy as jnp
from jax import lax
from jax.experimental import pallas as pl
from jax.experimental.pallas import tpu as pltpu
from jax.sharding import PartitionSpec as P

F32, BF16 = jnp.float32, jnp.bfloat16
MESH = pl.DeviceIdType.MESH
BIG = 16384.0
SCALE = math.sqrt(10.0 * math.log2(math.e))
LANES = 128
KN = 64
KC = 80


def nt(a, b):
    return lax.dot_general(a, b, (((1,), (1,)), ((), ())), preferred_element_type=F32)


def nn(a, b):
    return lax.dot_general(a, b, (((1,), (0,)), ((), ())), preferred_element_type=F32)


def iota(shape, dim):
    return lax.broadcasted_iota(jnp.int32, shape, dim)


def halves(x):
    hi = x.astype(BF16)
    return hi, (x - hi.astype(F32)).astype(BF16)


def stacked(x):
    hi = x.astype(BF16).astype(F32)
    return jnp.concatenate([hi, x - hi], axis=0).astype(BF16)


def folded(x):
    n = x.shape[0] // 2
    return x[:n] + x[n:]


def thirds(x):
    h = x.astype(BF16).astype(F32)
    m = (x - h).astype(BF16).astype(F32)
    return h, m, x - h - m


def source_rows(x):
    r = iota(x.shape, 0)
    x = jnp.where(r < 3, x, 0.0)
    n2 = jnp.sum(x * x, axis=0, keepdims=True)
    return jnp.where(r < 3, x, jnp.where(r == 3, n2, jnp.where(r == 4, 1.0, 0.0)))


def target_rows(x):
    r = iota(x.shape, 0)
    x = jnp.where(r < 3, x, 0.0)
    n2 = jnp.sum(x * x, axis=0, keepdims=True)
    return jnp.where(r < 3, 2.0 * x, jnp.where(r == 3, -1.0, jnp.where(r == 4, -n2, 0.0)))


def source_stack(rows):
    h, m, l = thirds(rows)
    return [h, m, l, h, m, h]


def target_stack(rows):
    h, m, l = thirds(rows)
    return [h, h, h, m, m, l]


def once(fn):
    fn()


def gauss(e):
    g = jnp.exp2(e)
    return halves(g)


def kernel(
    n_dev,
    pts_hbm, rhs_hbm, basis_hbm, tr_hbm, px_hbm, nl_hbm, cl_hbm, rl_hbm,
    out_ref,
    pts_ref, rhs_ref, basis_ref, tr_ref, px_ref, nl_ref, cl_ref, rl_ref, in_sem,
    nr, p8, pa, tb, tbh, tbl, eye_ref, bmask,
    ytn, chn, xn, ytc, chc, xc, xc1, clb, nlb, rb,
    gc, fc, fd,
    sn, rn, sl, rlr, s1, r1, sq, sq2, rq, rg,
    sem_s, sem_r, gs_sem, gr_sem,
):
    loads = {
        name: pltpu.make_async_copy(src, dst, in_sem.at[i])
        for i, (name, src, dst) in enumerate((
            ("px", px_hbm, px_ref), ("basis", basis_hbm, basis_ref), ("rhs", rhs_hbm, rhs_ref),
            ("tr", tr_hbm, tr_ref), ("pts", pts_hbm, pts_ref), ("nl", nl_hbm, nl_ref),
            ("cl", cl_hbm, cl_ref), ("rl", rl_hbm, rl_ref),
        ))
    }
    for c in loads.values():
        c.start()
    me = lax.axis_index("leaf")
    groups = n_dev // 8
    group, seat = me // 8, me % 8
    left, right = (me + n_dev - 1) % n_dev, (me + 1) % n_dev
    left2, right2 = (me + n_dev - 2) % n_dev, (me + 2) % n_dev
    peers = [group * 8 + (seat + o) % 8 for o in range(1, 8)]

    def dst(o):
        return ((group + o) % groups) * 8 + seat

    barrier = pltpu.get_barrier_semaphore()
    for d in [left, right, left2, right2, *peers]:
        pl.semaphore_signal(barrier, inc=1, device_id=(d,), device_id_type=MESH)

    def greet(o, c):
        pl.semaphore_signal(barrier, inc=1, device_id=(dst(o),), device_id_type=MESH)
        return c

    lax.fori_loop(1, groups, greet, 0)

    def sec_const():
        eye_ref[...] = jnp.where(iota((LANES, LANES), 0) == iota((LANES, LANES), 1), 1.0, 0.0).astype(BF16)
        bmask[...] = jnp.where(iota((LANES, 256), 0) // 32 == iota((LANES, 256), 1) // 64, 1.0, 0.0).astype(BF16)

    once(sec_const)

    loads["px"].wait()
    def sec_prox():
        pick = jnp.where(
            ((iota((24, 85), 1) >= 1) & ((iota((24, 85), 1) - 1) >> 2 == iota((24, 85), 0)))
            | ((iota((24, 85), 1) == 0) & (iota((24, 85), 0) == 21)), 1.0, 0.0).astype(BF16)
        lane_p, row_p = iota((LANES, 85), 1), iota((LANES, 85), 0)
        pmask = (lane_p == 0) | ((lane_p + 3) % 4 == (row_p >> 5))
        pa[...] = jnp.zeros_like(pa)
        for ax in range(3):
            w = (px_ref[ax] - 0.5) * SCALE
            w = jnp.where(pmask, jnp.concatenate([w, w, w, w], axis=0), 0.0)
            h, m, l = thirds(w)
            pa[pl.ds(ax, 24, stride=8), :] = (
                nt(pick, h.astype(BF16)) + nt(pick, m.astype(BF16)) + nt(pick, l.astype(BF16))
            )

    once(sec_prox)

    def basis_parts(q):
        hi, lo = halves(basis_ref[:, pl.ds(q * 256, 256)])
        mask = bmask[...]
        return (
            jnp.concatenate([hi, hi, hi, hi], axis=0) * mask,
            jnp.concatenate([lo, lo, lo, lo], axis=0) * mask,
        )

    loads["basis"].wait()
    loads["rhs"].wait()
    coef3 = gc

    def leaf_coef(q, c):
        bh, bl = basis_parts(q)
        v = stacked(rhs_ref[:, pl.ds(q * 256, 256)])
        coef3[5 + q] = folded(nt(v, bh) + nt(v, bl))
        return c


    loads["tr"].wait()
    lane_n, row_n = iota((LANES, 84), 1), iota((LANES, 84), 0)
    tmask = (lane_n < 4) | (((lane_n >> 2) + 3) % 4 == (row_n >> 5))
    tmask = jnp.where(tmask, 1.0, 0.0).astype(BF16)
    eye88 = jnp.where(iota((88, 84), 0) == iota((88, 84), 1), 1.0, 0.0).astype(BF16)

    bit = [(iota((8, LANES), 0) & k) == 0 for k in (1, 2, 4)]

    def turn(g, c):
        wide = []
        for i in range(8):
            w = tr_ref[8 * g + i]
            hi, lo = [jnp.concatenate([x, x, x, x], axis=0) * tmask for x in halves(w)]
            wide.append(nt(eye88, hi) + nt(eye88, lo))
        for n in range(0, 84, 8):
            v = [w[n : n + 8] for w in wide]
            for p, k in ((2, 4), (1, 2), (0, 1)):
                for i in range(8):
                    if not i & k:
                        x, y = v[i], v[i + k]
                        v[i] = jnp.where(bit[p], x, pltpu.roll(y, k, axis=0))
                        v[i + k] = jnp.where(bit[p], pltpu.roll(x, 8 - k, axis=0), y)
            for i in range(min(8, 84 - n)):
                tb[pl.ds(pl.multiple_of((n + i) * 32 + 8 * g, 8), 8), :] = v[i]
        for i in range(4):
            leaf_coef(4 * g + i, 0)
        return c

    lax.fori_loop(0, 4, turn, 0, unroll=4)

    def part(i, c):
        hi, lo = halves(tb[pl.ds(i * LANES, LANES), :])
        tbh[i] = hi
        tbl[i] = lo
        return c

    lax.fori_loop(0, 21, part, 0, unroll=3)

    def sec_up():
        def rise(first, to):
            b = jnp.concatenate([stacked(coef3[first + i]) for i in range(4)], axis=1)
            w = [t[first : first + 4].reshape(512, LANES) for t in (tbh, tbl)]
            coef3[to] = folded(nn(b, w[0]) + nn(b, w[1]))

        for r in range(4):
            rise(5 + 4 * r, 1 + r)
        rise(1, 0)
        b = stacked(coef3[0])
        sq[0:16, :] = folded(nn(b, tbh[0]) + nn(b, tbl[0]))

    once(sec_up)

    pl.semaphore_wait(barrier, 11 + groups - 1)

    def remote(src, dst_ref, i, d):
        return pltpu.make_async_remote_copy(
            src_ref=src, dst_ref=dst_ref, send_sem=sem_s.at[i], recv_sem=sem_r.at[i],
            device_id=(d,), device_id_type=MESH,
        )

    sq[16:19, :] = pa[21 * 8 : 21 * 8 + 3, :]
    rq[seat] = sq[...]
    group_copies = [
        pltpu.make_async_remote_copy(
            src_ref=sq, dst_ref=rq.at[seat], send_sem=sem_s.at[6 + o], recv_sem=sem_r.at[6 + seat],
            device_id=(peers[o],), device_id_type=MESH,
        )
        for o in range(7)
    ]
    for c in group_copies:
        c.start()
    def sec_pack():
        for i, (to_left, to_right) in enumerate(((5, 19), (6, 20), (1, 3), (2, 4), (0, 0))):
            for side, u in ((0, to_left), (1, to_right)):
                sl[side, i, 0:16, :] = coef3[u]
                sl[side, i, 16:24, :] = source_rows(pa[u * 8 : u * 8 + 8, :])
        s1[0:16, :] = coef3[0]
        s1[16:24, :] = source_rows(pa[0:8, :])

    once(sec_pack)

    level_copies = [
        remote(sl.at[0], rlr.at[1], 2, left),
        remote(sl.at[1], rlr.at[0], 3, right),
        remote(s1, r1.at[1], 4, left2),
        remote(s1, r1.at[0], 5, right2),
    ]
    for c in level_copies:
        c.start()

    loads["pts"].wait()
    p8[...] = jnp.zeros_like(p8)
    p8[0:3, :] = (pts_ref[...] - 0.5) * SCALE
    for i, u in ((0, 0), (1, 31)):
        sn[i, 0:16, :] = rhs_ref[:, u * LANES : (u + 1) * LANES]
        sn[i, 16:24, :] = source_rows(p8[:, u * LANES : (u + 1) * LANES])

    near_copies = [
        remote(sn.at[0], rn.at[1], 0, left),
        remote(sn.at[1], rn.at[0], 1, right),
    ]
    for c in near_copies:
        c.start()

    for name in ("nl", "cl", "rl"):
        loads[name].wait()

    clb[...] = jnp.full_like(clb, -BIG)
    clb[0:20, 0:84] = jnp.where(cl_ref[...] >= 0, 0.0, -BIG)
    nlb[...] = jnp.full_like(nlb, -BIG)
    nlb[0:5, 0:64] = jnp.where(nl_ref[...] >= 0, 0.0, -BIG)
    nb = nlb[...]
    h = iota((8, LANES), 1) % 4
    for k in range(1, 4):
        nb = jnp.where(h == k, pltpu.roll(nlb[...], k, axis=0), nb)
    nlb[...] = nb
    cb = clb[...]
    clb[...] = jnp.where((iota((32, LANES), 1) + 4) % 8 >= 4, pltpu.roll(cb, 4, axis=0), cb)
    c1b = cb
    sel8 = jnp.where(iota((LANES, 256), 0) == iota((LANES, 256), 1) >> 5, 1.0, 0.0).astype(BF16)
    sel4 = jnp.where(iota((LANES, 256), 0) == iota((LANES, 256), 1) >> 6, 1.0, 0.0).astype(BF16)
    selm = jnp.where(iota((LANES, LANES), 0) % 4 == iota((LANES, LANES), 1) >> 5, 1.0, 0.0).astype(BF16)
    rlist = jnp.where(rl_ref[...] >= 0, 0.0, -BIG) + jnp.zeros((32, LANES), F32)
    rlist = jnp.where(iota((32, LANES), 1) >> 2 == iota((32, LANES), 0), rlist, 0.0)
    rb[...] = nn(rlist.astype(BF16), selm)

    def near_source(slab, values, rows):
        cls = (2 * slab + (iota((8, LANES), 1) >> 6)) % 8
        hot = jnp.where(iota((8, LANES), 0) == cls, 1.0, 0.0)
        f = jnp.concatenate([*source_stack(rows), hot, jnp.zeros((8, LANES), F32)], axis=0)
        ytn[pl.ds(pl.multiple_of(slab * LANES, LANES), LANES), :] = nt(eye_ref[...], f.astype(BF16)).astype(BF16)
        chn[slab] = stacked(values)

    def near_prep(v, c):
        for i in range(2):
            at = pl.ds(pl.multiple_of((2 * v + i) * LANES, LANES), LANES)
            near_source(2 * v + i + 1, rhs_ref[:, at], source_rows(p8[:, at]))
        x = p8[:, pl.ds(pl.multiple_of(v * 256, 256), 256)]
        bias = pltpu.roll(pltpu.roll(nlb[...], (LANES - 4 * v) % LANES, axis=1), (4 * v) % 8, axis=0)
        bias = nn(bias.astype(BF16), sel4)
        xn[v] = jnp.concatenate(
            [*target_stack(target_rows(x)), bias, jnp.zeros((8, 256), F32)], axis=0).astype(BF16)
        return c

    lax.fori_loop(0, 16, near_prep, 0, unroll=4)

    def chunked(feats, first, targets, values, slab, chunks):
        acc = None
        for i in range(chunks):
            at = pl.ds(pl.multiple_of(first + i * 256, 256), 256)
            gh, gl = gauss(nn(feats[at, :], targets))
            b = jnp.concatenate([values[slab + 2 * i], values[slab + 2 * i + 1]], axis=1)
            y = nn(b, gh) + nn(b, gl)
            acc = y if acc is None else acc + y
        return folded(acc)

    def near_unit(v, c):
        y = chunked(ytn, v * 256, xn[v], chn, 2 * v, 2)
        nr[:, pl.ds(pl.multiple_of(v * 256, 256), 256)] = y
        return c

    lax.fori_loop(1, 7, near_unit, 0, unroll=3)

    for o in range(7):
        group_copies[o].wait_send()
    for o in range(1, 8):
        frm = (seat + o) % 8
        pltpu.make_async_remote_copy(
            src_ref=sq, dst_ref=rq.at[frm], send_sem=sem_s.at[6], recv_sem=sem_r.at[6 + frm],
            device_id=(left,), device_id_type=MESH,
        ).wait_recv()
    place = iota((19, LANES), 1) >> 5
    for i in range(2):
        blocks = [rq[4 * i + j] for j in range(4)]
        merged = blocks[3]
        for j in range(3):
            merged = jnp.where(place == j, blocks[j], merged)
        sq2[i] = merged
        rg[group, i] = merged

    def root_send(o, c):
        pltpu.make_async_remote_copy(
            src_ref=sq2, dst_ref=rg.at[group], send_sem=gs_sem.at[0], recv_sem=gr_sem.at[0],
            device_id=(dst(o),), device_id_type=MESH,
        ).start()
        return c

    lax.fori_loop(1, groups, root_send, 0)

    lax.fori_loop(7, 15, near_unit, 0, unroll=4)

    def level_source(slab, q_class, values, rows):
        cls = (4 * q_class + (iota((32, LANES), 1) >> 5)) % 32
        hot = jnp.where(iota((32, LANES), 0) == cls, 1.0, 0.0)
        f = jnp.concatenate([*source_stack(rows), hot], axis=0)
        at = slab * LANES if isinstance(slab, int) else pl.multiple_of(slab * LANES, LANES)
        ytc[pl.ds(at, LANES), :] = nt(eye_ref[...], f.astype(BF16)).astype(BF16)
        chc[slab] = stacked(values)

    def level_prep(w, c):
        q = jnp.where(w < 8, 2 * w, 2 * w - 16)
        u = q + jnp.where(w < 8, 5, 1)
        slab = q + jnp.where(w < 8, 2, 22)
        xs = [pa[pl.ds(pl.multiple_of((u + i) * 8, 8), 8), :] for i in range(2)]
        for i in range(2):
            level_source(slab + i, q + 2 + i, coef3[u + i], source_rows(xs[i]))
        bias = pltpu.roll(pltpu.roll(clb[...], (LANES - 4 * u) % LANES, axis=1), (4 * q) % 32, axis=0)
        bias = nn(bias.astype(BF16), sel8)
        xs = target_rows(jnp.concatenate(xs, axis=1))
        xc[w] = jnp.concatenate([*target_stack(xs), bias], axis=0).astype(BF16)
        return c

    lax.fori_loop(0, 10, level_prep, 0, unroll=5)
    level_source(30, 2, coef3[0], source_rows(pa[0:8, :]))
    bias = nn(c1b.astype(BF16), sel8[:, 0:LANES])
    xc1[...] = jnp.concatenate([*target_stack(target_rows(pa[0:8, :])), bias], axis=0).astype(BF16)
    for c in level_copies:
        c.wait()
    def sec_halo():
        for i in range(2):
            for first, k, n in ((0, 0, 16), (20, 2, 4)):
                level_source(first + i, i, rlr[0, k + i, 0:16, :], rlr[0, k + i, 16:24, :])
                level_source(first + 2 + n + i, 2 + n + i, rlr[1, k + i, 0:16, :], rlr[1, k + i, 16:24, :])
        for i, blk in ((0, r1[0]), (1, rlr[0, 4]), (3, rlr[1, 4]), (4, r1[1])):
            level_source(28 + i, i, blk[0:16], blk[16:24])

    once(sec_halo)

    def couple_unit(w, c):
        q = jnp.where(w < 8, 2 * w, 2 * w - 16)
        u = q + jnp.where(w < 8, 5, 1)
        slab = q + jnp.where(w < 8, 0, 20)
        g = chunked(ytc, slab * LANES, xc[w], chc, slab, 3)
        fc[u] = g[:, 0:LANES]
        fc[u + 1] = g[:, LANES:256]
        return c

    lax.fori_loop(0, 10, couple_unit, 0, unroll=5)
    def sec_l1():
        gh, gl = gauss(nn(ytc[28 * LANES : 33 * LANES, :], xc1[...]))
        b = jnp.concatenate([chc[28 + i] for i in range(5)], axis=1)
        fc[0] = folded(nn(b, gh) + nn(b, gl))

    once(sec_l1)

    for c in near_copies:
        c.wait()
    near_source(0, rn[0, 0:16, :], rn[0, 16:24, :])
    near_source(33, rn[1, 0:16, :], rn[1, 16:24, :])

    near_unit(0, 0)
    near_unit(15, 0)

    froot = jnp.concatenate(target_stack(target_rows(pa[21 * 8 : 22 * 8, :])), axis=0)
    troot = nt(eye_ref[0:32, :], froot.astype(BF16)).astype(BF16)

    if groups > 1:
        others = rg.at[pl.ds(0, groups - 1)]
        pltpu.make_async_copy(others, others, gr_sem.at[0]).wait()

    def sec_tail():
        batch = min(8, 2 * groups)

        def root_unit(i, acc):
            us = [(i * batch + j) // 2 for j in range(batch)]
            rows = jnp.concatenate([rg[u, j % 2, 16:19, :] for j, u in enumerate(us)], axis=1)
            rows = source_rows(jnp.concatenate([rows, jnp.zeros((5, rows.shape[1]), F32)], axis=0))
            f = jnp.concatenate(source_stack(rows), axis=0).astype(BF16)
            bias = jnp.concatenate([rb[pl.ds(i * batch + j, 1), :] for j in range(batch)], axis=1)
            gh, gl = gauss(nn(troot, f) + bias)
            v = stacked(jnp.concatenate([rg[u, j % 2, 0:16, :] for j, u in enumerate(us)], axis=1))
            return acc + nt(v, jnp.concatenate([gh, gl], axis=0))

        acc = jnp.zeros((32, 64), F32)
        for i in range(2 * groups // batch):
            acc = root_unit(i, acc)
        acc = folded(acc)
        f0 = jnp.concatenate([acc, jnp.zeros((16, 64), F32)], axis=1)

        def down(f, u):
            b = stacked(f)
            return fc[u] + folded(nt(b, tbh[u]) + nt(b, tbl[u]))

        f1 = stacked(down(f0, 0))
        w = [t[1:5].reshape(512, LANES) for t in (tbh, tbl)]
        f2 = folded(nt(f1, w[0]) + nt(f1, w[1]))
        for r in range(4):
            b = stacked(fc[1 + r] + f2[:, r * LANES : (r + 1) * LANES])
            w = [t[5 + 4 * r : 9 + 4 * r].reshape(512, LANES) for t in (tbh, tbl)]
            f3 = folded(nt(b, w[0]) + nt(b, w[1]))
            for i in range(4):
                fd[4 * r + i] = stacked(fc[5 + 4 * r + i] + f3[:, i * LANES : (i + 1) * LANES])

    once(sec_tail)

    def far(q, c):
        at = pl.ds(pl.multiple_of(q * 256, 256), 256)
        bh, bl = basis_parts(q)
        b = fd[q]
        out_ref[:, at] = nr[:, at] + folded(nn(b, bh) + nn(b, bl))
        return c

    lax.fori_loop(0, 16, far, 0, unroll=8)

    if groups > 1:
        others = rg.at[pl.ds(0, groups - 1)]
        pltpu.make_async_copy(others, others, gs_sem.at[0]).wait()


def body(n_dev, points, rhs, leaf_basis, transfer, proxies, near_list, couple_list, root_list):
    rlist = root_list
    if n_dev < LANES:
        rlist = jnp.pad(rlist, ((0, 0), (0, LANES - n_dev)))
    groups = n_dev // 8
    ins = [(3, 4096), (16, 4096), (32, 4096), (32, 32, 84), (3, 32, 85), (5, 64), (20, 84), (1, LANES)]
    scratch = [
        *[pltpu.VMEM(shape, F32 if i < 5 else jnp.int32) for i, shape in enumerate(ins)],
        pltpu.SemaphoreType.DMA((8,)),
        pltpu.VMEM((16, 4096), F32),
        pltpu.VMEM((8, 4096), F32),
        pltpu.VMEM((192, LANES), F32),
        pltpu.VMEM((84 * 32, LANES), F32),
        pltpu.VMEM((21, LANES, LANES), BF16),
        pltpu.VMEM((21, LANES, LANES), BF16),
        pltpu.VMEM((LANES, LANES), BF16),
        pltpu.VMEM((LANES, 256), BF16),
        pltpu.VMEM((34 * LANES, KN), BF16),
        pltpu.VMEM((34, 32, LANES), BF16),
        pltpu.VMEM((16, KN, 256), BF16),
        pltpu.VMEM((33 * LANES, KC), BF16),
        pltpu.VMEM((33, 32, LANES), BF16),
        pltpu.VMEM((10, KC, 256), BF16),
        pltpu.VMEM((KC, LANES), BF16),
        pltpu.VMEM((32, LANES), F32),
        pltpu.VMEM((8, LANES), F32),
        pltpu.VMEM((32, LANES), F32),
        pltpu.VMEM((21, 16, LANES), F32),
        pltpu.VMEM((21, 16, LANES), F32),
        pltpu.VMEM((16, 32, LANES), BF16),
        pltpu.VMEM((2, 24, LANES), F32),
        pltpu.VMEM((2, 24, LANES), F32),
        pltpu.VMEM((2, 5, 24, LANES), F32),
        pltpu.VMEM((2, 5, 24, LANES), F32),
        pltpu.VMEM((24, LANES), F32),
        pltpu.VMEM((2, 24, LANES), F32),
        pltpu.VMEM((19, LANES), F32),
        pltpu.VMEM((2, 19, LANES), F32),
        pltpu.VMEM((8, 19, LANES), F32),
        pltpu.VMEM((groups, 2, 19, LANES), F32),
        pltpu.SemaphoreType.DMA((14,)),
        pltpu.SemaphoreType.DMA((14,)),
        pltpu.SemaphoreType.DMA((1,)),
        pltpu.SemaphoreType.DMA((1,)),
    ]
    vmem = pl.BlockSpec(memory_space=pltpu.VMEM)
    return pl.pallas_call(
        functools.partial(kernel, n_dev),
        out_shape=jax.ShapeDtypeStruct(rhs.shape, F32),
        in_specs=[pl.BlockSpec(memory_space=pltpu.HBM)] * 8,
        out_specs=vmem,
        scratch_shapes=scratch,
        compiler_params=pltpu.CompilerParams(
            collective_id=0, has_side_effects=True, vmem_limit_bytes=60 * 2**20
        ),
        name="hmatvec",
    )(points, rhs, leaf_basis, transfer, proxies, near_list.T, couple_list.T, rlist)


def solution(mesh):
    n_dev = mesh.shape["leaf"]
    in_specs = (
        P(None, "leaf"), P(None, "leaf"), P(None, "leaf"), P(None, None, "leaf"), P(None, None, "leaf"),
        P("leaf", None), P("leaf", None), P("leaf", None),
    )
    return jax.shard_map(
        functools.partial(body, n_dev), mesh=mesh, in_specs=in_specs, out_specs=P(None, "leaf"), check_vma=False
    )
```

```python
import functools
import math

import jax
import jax.numpy as jnp
from jax import lax
from jax.experimental import pallas as pl
from jax.experimental.pallas import tpu as pltpu
from jax.sharding import PartitionSpec as P

F32, BF16 = jnp.float32, jnp.bfloat16
MESH = pl.DeviceIdType.MESH
BIG = 16384.0
SCALE = math.sqrt(10.0 * math.log2(math.e))
LANES = 128
KN = 64
KC = 80


def nt(a, b):
    return lax.dot_general(a, b, (((1,), (1,)), ((), ())), preferred_element_type=F32)


def nn(a, b):
    return lax.dot_general(a, b, (((1,), (0,)), ((), ())), preferred_element_type=F32)


def iota(shape, dim):
    return lax.broadcasted_iota(jnp.int32, shape, dim)


def halves(x):
    hi = x.astype(BF16)
    return hi, (x - hi.astype(F32)).astype(BF16)


def stacked(x):
    hi = x.astype(BF16).astype(F32)
    return jnp.concatenate([hi, x - hi], axis=0).astype(BF16)


def folded(x):
    n = x.shape[0] // 2
    return x[:n] + x[n:]


def thirds(x):
    h = x.astype(BF16).astype(F32)
    m = (x - h).astype(BF16).astype(F32)
    return h, m, x - h - m


def source_rows(x):
    r = iota(x.shape, 0)
    x = jnp.where(r < 3, x, 0.0)
    n2 = jnp.sum(x * x, axis=0, keepdims=True)
    return jnp.where(r < 3, x, jnp.where(r == 3, n2, jnp.where(r == 4, 1.0, 0.0)))


def target_rows(x):
    r = iota(x.shape, 0)
    x = jnp.where(r < 3, x, 0.0)
    n2 = jnp.sum(x * x, axis=0, keepdims=True)
    return jnp.where(r < 3, 2.0 * x, jnp.where(r == 3, -1.0, jnp.where(r == 4, -n2, 0.0)))


def source_stack(rows):
    h, m, l = thirds(rows)
    return [h, m, l, h, m, h]


def target_stack(rows):
    h, m, l = thirds(rows)
    return [h, h, h, m, m, l]


def once(fn):
    fn()


def gauss(e):
    g = jnp.exp2(e)
    return halves(g)


def kernel(
    n_dev,
    pts_hbm, rhs_hbm, basis_hbm, tr_hbm, px_hbm, nl_hbm, cl_hbm, rl_hbm,
    out_ref,
    pts_ref, rhs_ref, basis_ref, tr_ref, px_ref, nl_ref, cl_ref, rl_ref, in_sem,
    nr, p8, pa, tb, tbh, tbl, eye_ref, bmask,
    ytn, chn, xn, ytc, chc, xc, xc1, clb, nlb, rb,
    gc, fc, fd,
    sn, rn, sl, rlr, s1, r1, sq, sq2, rq, rg,
    sem_s, sem_r, gs_sem, gr_sem,
):
    loads = {
        name: pltpu.make_async_copy(src, dst, in_sem.at[i])
        for i, (name, src, dst) in enumerate((
            ("px", px_hbm, px_ref), ("basis", basis_hbm, basis_ref), ("rhs", rhs_hbm, rhs_ref),
            ("tr", tr_hbm, tr_ref), ("pts", pts_hbm, pts_ref), ("nl", nl_hbm, nl_ref),
            ("cl", cl_hbm, cl_ref), ("rl", rl_hbm, rl_ref),
        ))
    }
    for c in loads.values():
        c.start()
    me = lax.axis_index("leaf")
    groups = n_dev // 8
    group, seat = me // 8, me % 8
    left, right = (me + n_dev - 1) % n_dev, (me + 1) % n_dev
    left2, right2 = (me + n_dev - 2) % n_dev, (me + 2) % n_dev
    peers = [group * 8 + (seat + o) % 8 for o in range(1, 8)]

    def dst(o):
        return ((group + o) % groups) * 8 + seat

    barrier = pltpu.get_barrier_semaphore()
    for d in [left, right, left2, right2, *peers]:
        pl.semaphore_signal(barrier, inc=1, device_id=(d,), device_id_type=MESH)

    def greet(o, c):
        pl.semaphore_signal(barrier, inc=1, device_id=(dst(o),), device_id_type=MESH)
        return c

    lax.fori_loop(1, groups, greet, 0)

    def sec_const():
        eye_ref[...] = jnp.where(iota((LANES, LANES), 0) == iota((LANES, LANES), 1), 1.0, 0.0).astype(BF16)
        bmask[...] = jnp.where(iota((LANES, 256), 0) // 32 == iota((LANES, 256), 1) // 64, 1.0, 0.0).astype(BF16)

    once(sec_const)

    loads["px"].wait()
    def sec_prox():
        pick = jnp.where(
            ((iota((24, 85), 1) >= 1) & ((iota((24, 85), 1) - 1) >> 2 == iota((24, 85), 0)))
            | ((iota((24, 85), 1) == 0) & (iota((24, 85), 0) == 21)), 1.0, 0.0).astype(BF16)
        lane_p, row_p = iota((LANES, 85), 1), iota((LANES, 85), 0)
        pmask = (lane_p == 0) | ((lane_p + 3) % 4 == (row_p >> 5))
        pa[...] = jnp.zeros_like(pa)
        for ax in range(3):
            w = (px_ref[ax] - 0.5) * SCALE
            w = jnp.where(pmask, jnp.concatenate([w, w, w, w], axis=0), 0.0)
            h, m, l = thirds(w)
            pa[pl.ds(ax, 24, stride=8), :] = (
                nt(pick, h.astype(BF16)) + nt(pick, m.astype(BF16)) + nt(pick, l.astype(BF16))
            )

    once(sec_prox)

    def basis_parts(q):
        hi, lo = halves(basis_ref[:, pl.ds(q * 256, 256)])
        mask = bmask[...]
        return (
            jnp.concatenate([hi, hi, hi, hi], axis=0) * mask,
            jnp.concatenate([lo, lo, lo, lo], axis=0) * mask,
        )

    loads["basis"].wait()
    loads["rhs"].wait()
    coef3 = gc

    def leaf_coef(q, c):
        bh, bl = basis_parts(q)
        v = stacked(rhs_ref[:, pl.ds(q * 256, 256)])
        coef3[5 + q] = folded(nt(v, bh) + nt(v, bl))
        return c


    loads["tr"].wait()
    lane_n, row_n = iota((LANES, 84), 1), iota((LANES, 84), 0)
    tmask = (lane_n < 4) | (((lane_n >> 2) + 3) % 4 == (row_n >> 5))
    tmask = jnp.where(tmask, 1.0, 0.0).astype(BF16)
    eye88 = jnp.where(iota((88, 84), 0) == iota((88, 84), 1), 1.0, 0.0).astype(BF16)

    bit = [(iota((8, LANES), 0) & k) == 0 for k in (1, 2, 4)]

    def turn(g, c):
        wide = []
        for i in range(8):
            w = tr_ref[8 * g + i]
            hi, lo = [jnp.concatenate([x, x, x, x], axis=0) * tmask for x in halves(w)]
            wide.append(nt(eye88, hi) + nt(eye88, lo))
        for n in range(0, 84, 8):
            v = [w[n : n + 8] for w in wide]
            for p, k in ((2, 4), (1, 2), (0, 1)):
                for i in range(8):
                    if not i & k:
                        x, y = v[i], v[i + k]
                        v[i] = jnp.where(bit[p], x, pltpu.roll(y, k, axis=0))
                        v[i + k] = jnp.where(bit[p], pltpu.roll(x, 8 - k, axis=0), y)
            for i in range(min(8, 84 - n)):
                tb[pl.ds(pl.multiple_of((n + i) * 32 + 8 * g, 8), 8), :] = v[i]
        for i in range(4):
            leaf_coef(4 * g + i, 0)
        return c

    lax.fori_loop(0, 4, turn, 0, unroll=4)

    def part(i, c):
        hi, lo = halves(tb[pl.ds(i * LANES, LANES), :])
        tbh[i] = hi
        tbl[i] = lo
        return c

    lax.fori_loop(0, 21, part, 0, unroll=7)

    def sec_up():
        def rise(first, to):
            b = jnp.concatenate([stacked(coef3[first + i]) for i in range(4)], axis=1)
            w = [t[first : first + 4].reshape(512, LANES) for t in (tbh, tbl)]
            coef3[to] = folded(nn(b, w[0]) + nn(b, w[1]))

        for r in range(4):
            rise(5 + 4 * r, 1 + r)
        rise(1, 0)
        b = stacked(coef3[0])
        sq[0:16, :] = folded(nn(b, tbh[0]) + nn(b, tbl[0]))

    once(sec_up)

    pl.semaphore_wait(barrier, 11 + groups - 1)

    def remote(src, dst_ref, i, d):
        return pltpu.make_async_remote_copy(
            src_ref=src, dst_ref=dst_ref, send_sem=sem_s.at[i], recv_sem=sem_r.at[i],
            device_id=(d,), device_id_type=MESH,
        )

    sq[16:19, :] = pa[21 * 8 : 21 * 8 + 3, :]
    rq[seat] = sq[...]
    group_copies = [
        pltpu.make_async_remote_copy(
            src_ref=sq, dst_ref=rq.at[seat], send_sem=sem_s.at[6 + o], recv_sem=sem_r.at[6 + seat],
            device_id=(peers[o],), device_id_type=MESH,
        )
        for o in range(7)
    ]
    for c in group_copies:
        c.start()
    def sec_pack():
        for i, (to_left, to_right) in enumerate(((5, 19), (6, 20), (1, 3), (2, 4), (0, 0))):
            for side, u in ((0, to_left), (1, to_right)):
                sl[side, i, 0:16, :] = coef3[u]
                sl[side, i, 16:24, :] = source_rows(pa[u * 8 : u * 8 + 8, :])
        s1[0:16, :] = coef3[0]
        s1[16:24, :] = source_rows(pa[0:8, :])

    once(sec_pack)

    level_copies = [
        remote(sl.at[0], rlr.at[1], 2, left),
        remote(sl.at[1], rlr.at[0], 3, right),
        remote(s1, r1.at[1], 4, left2),
        remote(s1, r1.at[0], 5, right2),
    ]
    for c in level_copies:
        c.start()

    loads["pts"].wait()
    p8[...] = jnp.zeros_like(p8)
    p8[0:3, :] = (pts_ref[...] - 0.5) * SCALE
    for i, u in ((0, 0), (1, 31)):
        sn[i, 0:16, :] = rhs_ref[:, u * LANES : (u + 1) * LANES]
        sn[i, 16:24, :] = source_rows(p8[:, u * LANES : (u + 1) * LANES])

    near_copies = [
        remote(sn.at[0], rn.at[1], 0, left),
        remote(sn.at[1], rn.at[0], 1, right),
    ]
    for c in near_copies:
        c.start()

    for name in ("nl", "cl", "rl"):
        loads[name].wait()

    clb[...] = jnp.full_like(clb, -BIG)
    clb[0:20, 0:84] = jnp.where(cl_ref[...] >= 0, 0.0, -BIG)
    nlb[...] = jnp.full_like(nlb, -BIG)
    nlb[0:5, 0:64] = jnp.where(nl_ref[...] >= 0, 0.0, -BIG)
    nb = nlb[...]
    h = iota((8, LANES), 1) % 4
    for k in range(1, 4):
        nb = jnp.where(h == k, pltpu.roll(nlb[...], k, axis=0), nb)
    nlb[...] = nb
    cb = clb[...]
    clb[...] = jnp.where((iota((32, LANES), 1) + 4) % 8 >= 4, pltpu.roll(cb, 4, axis=0), cb)
    c1b = cb
    sel8 = jnp.where(iota((LANES, 256), 0) == iota((LANES, 256), 1) >> 5, 1.0, 0.0).astype(BF16)
    sel4 = jnp.where(iota((LANES, 256), 0) == iota((LANES, 256), 1) >> 6, 1.0, 0.0).astype(BF16)
    selm = jnp.where(iota((LANES, LANES), 0) % 4 == iota((LANES, LANES), 1) >> 5, 1.0, 0.0).astype(BF16)
    rlist = jnp.where(rl_ref[...] >= 0, 0.0, -BIG) + jnp.zeros((32, LANES), F32)
    rlist = jnp.where(iota((32, LANES), 1) >> 2 == iota((32, LANES), 0), rlist, 0.0)
    rb[...] = nn(rlist.astype(BF16), selm)

    def near_source(slab, values, rows):
        cls = (2 * slab + (iota((8, LANES), 1) >> 6)) % 8
        hot = jnp.where(iota((8, LANES), 0) == cls, 1.0, 0.0)
        f = jnp.concatenate([*source_stack(rows), hot, jnp.zeros((8, LANES), F32)], axis=0)
        ytn[pl.ds(pl.multiple_of(slab * LANES, LANES), LANES), :] = nt(eye_ref[...], f.astype(BF16)).astype(BF16)
        chn[slab] = stacked(values)

    def near_prep(v, c):
        for i in range(2):
            at = pl.ds(pl.multiple_of((2 * v + i) * LANES, LANES), LANES)
            near_source(2 * v + i + 1, rhs_ref[:, at], source_rows(p8[:, at]))
        x = p8[:, pl.ds(pl.multiple_of(v * 256, 256), 256)]
        bias = pltpu.roll(pltpu.roll(nlb[...], (LANES - 4 * v) % LANES, axis=1), (4 * v) % 8, axis=0)
        bias = nn(bias.astype(BF16), sel4)
        xn[v] = jnp.concatenate(
            [*target_stack(target_rows(x)), bias, jnp.zeros((8, 256), F32)], axis=0).astype(BF16)
        return c

    lax.fori_loop(0, 16, near_prep, 0, unroll=4)

    def chunked(feats, first, targets, values, slab, chunks):
        acc = None
        for i in range(chunks):
            at = pl.ds(pl.multiple_of(first + i * 256, 256), 256)
            gh, gl = gauss(nn(feats[at, :], targets))
            b = jnp.concatenate([values[slab + 2 * i], values[slab + 2 * i + 1]], axis=1)
            y = nn(b, gh) + nn(b, gl)
            acc = y if acc is None else acc + y
        return folded(acc)

    def near_unit(v, c):
        y = chunked(ytn, v * 256, xn[v], chn, 2 * v, 2)
        nr[:, pl.ds(pl.multiple_of(v * 256, 256), 256)] = y
        return c

    lax.fori_loop(1, 7, near_unit, 0, unroll=6)

    for o in range(7):
        group_copies[o].wait_send()
    for o in range(1, 8):
        frm = (seat + o) % 8
        pltpu.make_async_remote_copy(
            src_ref=sq, dst_ref=rq.at[frm], send_sem=sem_s.at[6], recv_sem=sem_r.at[6 + frm],
            device_id=(left,), device_id_type=MESH,
        ).wait_recv()
    place = iota((19, LANES), 1) >> 5
    for i in range(2):
        blocks = [rq[4 * i + j] for j in range(4)]
        merged = blocks[3]
        for j in range(3):
            merged = jnp.where(place == j, blocks[j], merged)
        sq2[i] = merged
        rg[group, i] = merged

    def root_send(o, c):
        pltpu.make_async_remote_copy(
            src_ref=sq2, dst_ref=rg.at[group], send_sem=gs_sem.at[0], recv_sem=gr_sem.at[0],
            device_id=(dst(o),), device_id_type=MESH,
        ).start()
        return c

    lax.fori_loop(1, groups, root_send, 0)

    lax.fori_loop(7, 15, near_unit, 0, unroll=4)

    def level_source(slab, q_class, values, rows):
        cls = (4 * q_class + (iota((32, LANES), 1) >> 5)) % 32
        hot = jnp.where(iota((32, LANES), 0) == cls, 1.0, 0.0)
        f = jnp.concatenate([*source_stack(rows), hot], axis=0)
        at = slab * LANES if isinstance(slab, int) else pl.multiple_of(slab * LANES, LANES)
        ytc[pl.ds(at, LANES), :] = nt(eye_ref[...], f.astype(BF16)).astype(BF16)
        chc[slab] = stacked(values)

    def level_prep(w, c):
        q = jnp.where(w < 8, 2 * w, 2 * w - 16)
        u = q + jnp.where(w < 8, 5, 1)
        slab = q + jnp.where(w < 8, 2, 22)
        xs = [pa[pl.ds(pl.multiple_of((u + i) * 8, 8), 8), :] for i in range(2)]
        for i in range(2):
            level_source(slab + i, q + 2 + i, coef3[u + i], source_rows(xs[i]))
        bias = pltpu.roll(pltpu.roll(clb[...], (LANES - 4 * u) % LANES, axis=1), (4 * q) % 32, axis=0)
        bias = nn(bias.astype(BF16), sel8)
        xs = target_rows(jnp.concatenate(xs, axis=1))
        xc[w] = jnp.concatenate([*target_stack(xs), bias], axis=0).astype(BF16)
        return c

    lax.fori_loop(0, 10, level_prep, 0, unroll=5)
    level_source(30, 2, coef3[0], source_rows(pa[0:8, :]))
    bias = nn(c1b.astype(BF16), sel8[:, 0:LANES])
    xc1[...] = jnp.concatenate([*target_stack(target_rows(pa[0:8, :])), bias], axis=0).astype(BF16)
    for c in level_copies:
        c.wait()
    def sec_halo():
        for i in range(2):
            for first, k, n in ((0, 0, 16), (20, 2, 4)):
                level_source(first + i, i, rlr[0, k + i, 0:16, :], rlr[0, k + i, 16:24, :])
                level_source(first + 2 + n + i, 2 + n + i, rlr[1, k + i, 0:16, :], rlr[1, k + i, 16:24, :])
        for i, blk in ((0, r1[0]), (1, rlr[0, 4]), (3, rlr[1, 4]), (4, r1[1])):
            level_source(28 + i, i, blk[0:16], blk[16:24])

    once(sec_halo)

    def couple_unit(w, c):
        q = jnp.where(w < 8, 2 * w, 2 * w - 16)
        u = q + jnp.where(w < 8, 5, 1)
        slab = q + jnp.where(w < 8, 0, 20)
        g = chunked(ytc, slab * LANES, xc[w], chc, slab, 3)
        fc[u] = g[:, 0:LANES]
        fc[u + 1] = g[:, LANES:256]
        return c

    lax.fori_loop(0, 10, couple_unit, 0, unroll=5)
    def sec_l1():
        gh, gl = gauss(nn(ytc[28 * LANES : 33 * LANES, :], xc1[...]))
        b = jnp.concatenate([chc[28 + i] for i in range(5)], axis=1)
        fc[0] = folded(nn(b, gh) + nn(b, gl))

    once(sec_l1)

    for c in near_copies:
        c.wait()
    near_source(0, rn[0, 0:16, :], rn[0, 16:24, :])
    near_source(33, rn[1, 0:16, :], rn[1, 16:24, :])

    near_unit(0, 0)
    near_unit(15, 0)

    froot = jnp.concatenate(target_stack(target_rows(pa[21 * 8 : 22 * 8, :])), axis=0)
    troot = nt(eye_ref[0:32, :], froot.astype(BF16)).astype(BF16)

    if groups > 1:
        others = rg.at[pl.ds(0, groups - 1)]
        pltpu.make_async_copy(others, others, gr_sem.at[0]).wait()

    def sec_tail():
        batch = min(8, 2 * groups)

        def root_unit(i, acc):
            us = [(i * batch + j) // 2 for j in range(batch)]
            rows = jnp.concatenate([rg[u, j % 2, 16:19, :] for j, u in enumerate(us)], axis=1)
            rows = source_rows(jnp.concatenate([rows, jnp.zeros((5, rows.shape[1]), F32)], axis=0))
            f = jnp.concatenate(source_stack(rows), axis=0).astype(BF16)
            bias = jnp.concatenate([rb[pl.ds(i * batch + j, 1), :] for j in range(batch)], axis=1)
            gh, gl = gauss(nn(troot, f) + bias)
            v = stacked(jnp.concatenate([rg[u, j % 2, 0:16, :] for j, u in enumerate(us)], axis=1))
            return acc + nt(v, jnp.concatenate([gh, gl], axis=0))

        acc = jnp.zeros((32, 64), F32)
        for i in range(2 * groups // batch):
            acc = root_unit(i, acc)
        acc = folded(acc)
        f0 = jnp.concatenate([acc, jnp.zeros((16, 64), F32)], axis=1)

        def down(f, u):
            b = stacked(f)
            return fc[u] + folded(nt(b, tbh[u]) + nt(b, tbl[u]))

        f1 = stacked(down(f0, 0))
        w = [t[1:5].reshape(512, LANES) for t in (tbh, tbl)]
        f2 = folded(nt(f1, w[0]) + nt(f1, w[1]))
        for r in range(4):
            b = stacked(fc[1 + r] + f2[:, r * LANES : (r + 1) * LANES])
            w = [t[5 + 4 * r : 9 + 4 * r].reshape(512, LANES) for t in (tbh, tbl)]
            f3 = folded(nt(b, w[0]) + nt(b, w[1]))
            for i in range(4):
                fd[4 * r + i] = stacked(fc[5 + 4 * r + i] + f3[:, i * LANES : (i + 1) * LANES])

    once(sec_tail)

    def far(q, c):
        at = pl.ds(pl.multiple_of(q * 256, 256), 256)
        bh, bl = basis_parts(q)
        b = fd[q]
        out_ref[:, at] = nr[:, at] + folded(nn(b, bh) + nn(b, bl))
        return c

    lax.fori_loop(0, 16, far, 0, unroll=8)

    if groups > 1:
        others = rg.at[pl.ds(0, groups - 1)]
        pltpu.make_async_copy(others, others, gs_sem.at[0]).wait()


def body(n_dev, points, rhs, leaf_basis, transfer, proxies, near_list, couple_list, root_list):
    rlist = root_list
    if n_dev < LANES:
        rlist = jnp.pad(rlist, ((0, 0), (0, LANES - n_dev)))
    groups = n_dev // 8
    ins = [(3, 4096), (16, 4096), (32, 4096), (32, 32, 84), (3, 32, 85), (5, 64), (20, 84), (1, LANES)]
    scratch = [
        *[pltpu.VMEM(shape, F32 if i < 5 else jnp.int32) for i, shape in enumerate(ins)],
        pltpu.SemaphoreType.DMA((8,)),
        pltpu.VMEM((16, 4096), F32),
        pltpu.VMEM((8, 4096), F32),
        pltpu.VMEM((192, LANES), F32),
        pltpu.VMEM((84 * 32, LANES), F32),
        pltpu.VMEM((21, LANES, LANES), BF16),
        pltpu.VMEM((21, LANES, LANES), BF16),
        pltpu.VMEM((LANES, LANES), BF16),
        pltpu.VMEM((LANES, 256), BF16),
        pltpu.VMEM((34 * LANES, KN), BF16),
        pltpu.VMEM((34, 32, LANES), BF16),
        pltpu.VMEM((16, KN, 256), BF16),
        pltpu.VMEM((33 * LANES, KC), BF16),
        pltpu.VMEM((33, 32, LANES), BF16),
        pltpu.VMEM((10, KC, 256), BF16),
        pltpu.VMEM((KC, LANES), BF16),
        pltpu.VMEM((32, LANES), F32),
        pltpu.VMEM((8, LANES), F32),
        pltpu.VMEM((32, LANES), F32),
        pltpu.VMEM((21, 16, LANES), F32),
        pltpu.VMEM((21, 16, LANES), F32),
        pltpu.VMEM((16, 32, LANES), BF16),
        pltpu.VMEM((2, 24, LANES), F32),
        pltpu.VMEM((2, 24, LANES), F32),
        pltpu.VMEM((2, 5, 24, LANES), F32),
        pltpu.VMEM((2, 5, 24, LANES), F32),
        pltpu.VMEM((24, LANES), F32),
        pltpu.VMEM((2, 24, LANES), F32),
        pltpu.VMEM((19, LANES), F32),
        pltpu.VMEM((2, 19, LANES), F32),
        pltpu.VMEM((8, 19, LANES), F32),
        pltpu.VMEM((groups, 2, 19, LANES), F32),
        pltpu.SemaphoreType.DMA((14,)),
        pltpu.SemaphoreType.DMA((14,)),
        pltpu.SemaphoreType.DMA((1,)),
        pltpu.SemaphoreType.DMA((1,)),
    ]
    vmem = pl.BlockSpec(memory_space=pltpu.VMEM)
    return pl.pallas_call(
        functools.partial(kernel, n_dev),
        out_shape=jax.ShapeDtypeStruct(rhs.shape, F32),
        in_specs=[pl.BlockSpec(memory_space=pltpu.HBM)] * 8,
        out_specs=vmem,
        scratch_shapes=scratch,
        compiler_params=pltpu.CompilerParams(
            collective_id=0, has_side_effects=True, vmem_limit_bytes=60 * 2**20
        ),
        name="hmatvec",
    )(points, rhs, leaf_basis, transfer, proxies, near_list.T, couple_list.T, rlist)


def solution(mesh):
    n_dev = mesh.shape["leaf"]
    in_specs = (
        P(None, "leaf"), P(None, "leaf"), P(None, "leaf"), P(None, None, "leaf"), P(None, None, "leaf"),
        P("leaf", None), P("leaf", None), P("leaf", None),
    )
    return jax.shard_map(
        functools.partial(body, n_dev), mesh=mesh, in_specs=in_specs, out_specs=P(None, "leaf"), check_vma=False
    )
```
